32 devices in a mesh: roll: 16 (over z, y, x), exp: 2 (over core).
Axes of the slice: x: 2, y: 2, z: 4, core: 2. Of those that a mesh axis runs over, the one named last changes fastest.
Arguments:
- kda_prefill: bfloat16 [64, 32, 128, 128], P('roll', 'exp'), may hold values from -6 to 6
- latent_prefill: bfloat16 [64, 64, 576], P('roll', 'exp'), may hold values from -6 to 6
- prompt_len: int32 [64], replicated, may hold values from 1 to 64, as said below
- sample_counts: int32 [16, 4], replicated, may hold values from 1 to 16, 32 in all within a row
- kda_q: bfloat16 [2, 512, 4096], P(None, 'roll', 'exp'), may hold values from -6 to 6
- kda_k: bfloat16 [2, 512, 4096], P(None, 'roll', 'exp'), may hold values from -6 to 6
- kda_v: bfloat16 [2, 512, 4096], P(None, 'roll', 'exp'), may hold values from -6 to 6
- kda_decay: float32 [2, 512, 4096], P(None, 'roll', 'exp'), may hold values from 0.005 to 0.5
- kda_beta: float32 [2, 512, 32], P(None, 'roll', 'exp'), may hold values from 0.1 to 0.9
- mla_q: bfloat16 [2, 512, 18432], P(None, 'roll', 'exp'), may hold values from -6 to 6
- mla_new: bfloat16 [2, 512, 576], P(None, 'roll'), may hold values from -6 to 6
- w_uv: bfloat16 [32, 512, 128], P('exp'), may hold values from -0.25 to 0.25
Outputs:
- kda_out: bfloat16 [2, 512, 4096], P(None, 'roll', 'exp')
- mla_out: bfloat16 [2, 512, 4096], P(None, 'roll', 'exp')
The draws below stay inside these ranges and needn't reach their ends.
Inputs may be any that keep to these rules, and one draw needn't show every extreme that they name: `prompt_len`: some prompt has length 1 and some has 64. `sample_counts`: each owner's row sums to 32; some prompt has 16 samples.
All inputs are finite; a program needn't handle non-finite values.
Results may differ from the reference program's by a relative error of at most 0.0057.
Values may be sent and summed in bfloat16 or wider, within the bound.
No kernel may reach another device: no remote copies, remote signals or barrier semaphores. Data moves between devices by JAX's collectives and lax.ppermute only.
A program may use at most 128 MiB of HBM per device.

```python
import math
import jax
import jax.numpy as jnp
import numpy as np
from jax import lax

H = 32
DK = 128
DV = 128
R = 512
RR = 64
MOST = 16
STEPS = 2
S_DEV = 32
P_DEV = 4
L = 64
OWNERS = 16
PROMPTS = 64
SAMPLES = 512
RC = 576


def draw_prompt_len(key, part):
    key = jax.random.fold_in(key, 11)
    drawn = jax.random.randint(key, (PROMPTS,), 1, L + 1, dtype=jnp.int32)
    drawn = drawn.at[0].set(L)
    return drawn.at[1].set(1)


def draw_mla_new(key, part):
    key = jax.random.fold_in(key, 12)
    return jnp.clip(jax.random.normal(key, (STEPS, SAMPLES, RC), jnp.float32), -6.0, 6.0).astype(jnp.bfloat16)


def draw_mla_q(key, part):
    key = jax.random.fold_in(key, 13)
    return jnp.clip(jax.random.normal(key, (STEPS, SAMPLES, H * RC), jnp.float32), -6.0, 6.0).astype(jnp.bfloat16)


def shard_levels(rng, shape, shards, low, largest):
    def one(dim, blocks):
        heights = jax.random.uniform(jax.random.fold_in(jax.random.fold_in(rng, 6), dim), (blocks,), jnp.float32, low / len(shards), largest / len(shards))
        return jnp.repeat(jnp.exp(heights), shape[dim] // blocks).reshape((-1,) + (1,) * (len(shape) - dim - 1))

    loudness = one(*shards[0])
    for cut in shards[1:]:
        loudness = loudness * one(*cut)
    return loudness


def split_up(number_of, total, limit, slope):
    portions = [(1 << 20) // math.isqrt(standing ** slope) + 1 for standing in range(2, number_of + 1)]
    rest, given = total - limit - (number_of - 1), [1] * (number_of - 1)
    while rest > 0:
        movable = [i for i in range(number_of - 1) if given[i] < limit]
        mass, left = sum([portions[i] for i in movable]), rest
        for i in movable:
            more = min(limit - given[i], max(1, left * portions[i] // mass), rest)
            given[i] = given[i] + more
            rest = rest - more
    return np.array([limit] + given)


def uneven_parts(stream_key, amount, total, most, lean):
    if amount == 2:
        one = jax.random.randint(stream_key, (), max(1, total - most), min(most, total - 1) + 1)
        return jnp.stack([one, total - one])
    tallies = jnp.asarray(split_up(amount, total, most, lean), jnp.int32)
    couples = (amount - 1) // 2
    giver, receiver = tallies[1:1 + 2 * couples:2], tallies[2:2 + 2 * couples:2]
    room = jnp.minimum(giver - 1, most - receiver)
    passed = jax.random.randint(jax.random.fold_in(stream_key, 1), (couples,), 0, 1 << 20) % (room + 1)
    tallies = tallies.at[1:1 + 2 * couples:2].set(giver - passed).at[2:2 + 2 * couples:2].set(receiver + passed)
    return tallies[jax.random.permutation(jax.random.fold_in(stream_key, 2), amount)]


def bell_draw(rng, extent, spread, limit, cuts=(), kind=jnp.bfloat16):
    entries = spread * jax.random.normal(rng, extent, jnp.float32)
    if cuts:
        entries = entries * shard_levels(rng, extent, cuts, -0.22, 0.18)
    return jnp.clip(entries, -limit, limit).astype(kind)


def setup_inputs(seed: int = 0) -> dict:
    arg_keys = jax.random.split(jax.random.key(seed), 13)
    return {
        "kda_prefill": bell_draw(arg_keys[0], (PROMPTS, H, DK, DV), 1.0, 6.0, ((0, 16), (1, 2))),
        "latent_prefill": bell_draw(arg_keys[1], (PROMPTS, L, RC), 1.0, 6.0, ((0, 16), (1, 2))),
        "prompt_len": draw_prompt_len(jax.random.fold_in(arg_keys[12], 71), 0),
        "sample_counts": jax.vmap(lambda own: uneven_parts(own, P_DEV, S_DEV, MOST, 2))(jax.random.split(arg_keys[3], OWNERS)).reshape((OWNERS, P_DEV)).astype(jnp.int32),
        "kda_q": bell_draw(arg_keys[4], (STEPS, SAMPLES, H * DK), 1.0, 6.0, ((1, 16), (2, 2))),
        "kda_k": bell_draw(arg_keys[5], (STEPS, SAMPLES, H * DK), 1.0, 6.0, ((1, 16), (2, 2))),
        "kda_v": bell_draw(arg_keys[6], (STEPS, SAMPLES, H * DV), 1.0, 6.0, ((1, 16), (2, 2))),
        "kda_decay": jnp.clip(jnp.exp(math.log(0.5) - 4.6051702 * jax.random.uniform(arg_keys[7], (STEPS, SAMPLES, H * DK), jnp.float32) ** shard_levels(arg_keys[7], (STEPS, SAMPLES, H * DK), ((1, 16), (2, 2)), -0.2, 0.2)), 0.005, 0.5),
        "kda_beta": jnp.clip(0.1 + 0.79999997 * jax.random.uniform(arg_keys[8], (STEPS, SAMPLES, H), jnp.float32) ** shard_levels(arg_keys[8], (STEPS, SAMPLES, H), ((1, 16), (2, 2)), -0.2, 0.2), 0.1, 0.9),
        "mla_q": draw_mla_q(jax.random.fold_in(arg_keys[12], 71), 0),
        "mla_new": draw_mla_new(jax.random.fold_in(arg_keys[12], 71), 0),
        "w_uv": bell_draw(arg_keys[11], (H, R, DV), R ** -0.5, 0.25, ((0, 2),)),
    }


def unit_rows(values):
    return values * lax.rsqrt(lax.optimization_barrier(jnp.sum(values * values, axis=-1, keepdims=True)) + 1e-06)

def delta_run(state, query_all, key_all, value_all, decay_all, beta_all):
    batch, heads, key_dim, value_dim = state.shape
    outputs = []
    for step_index in range(query_all.shape[0]):
        query_now = unit_rows(query_all[step_index].astype(jnp.float32).reshape(batch, heads, key_dim))
        key_now = unit_rows(key_all[step_index].astype(jnp.float32).reshape(batch, heads, key_dim))
        value_now = value_all[step_index].astype(jnp.float32).reshape(batch, heads, value_dim)
        keep_rate = jnp.exp(-decay_all[step_index].reshape(batch, heads, key_dim))
        beta_now = beta_all[step_index]
        state = state * keep_rate[..., None]
        guess = jnp.einsum('bhkv,bhk->bhv', state, key_now, precision=lax.Precision.HIGHEST)
        state = state + beta_now[..., None, None] * key_now[..., None] * (value_now - guess)[..., None, :]
        reading = jnp.einsum('bhkv,bhk->bhv', state, query_now, precision=lax.Precision.HIGHEST)
        outputs.append(reading.reshape(batch, heads * value_dim).astype(jnp.bfloat16))
    return jnp.stack(outputs)

def latent_run(cache, cache_lengths, query_all, fresh_all, up_value):
    batch, cache_len, width = cache.shape
    step_count = query_all.shape[0]
    heads, rank, value_dim = up_value.shape
    keys_all = jnp.concatenate([cache, jnp.swapaxes(fresh_all, 0, 1)], axis=1)
    prompt_valid = jnp.arange(cache_len, dtype=jnp.int32)[None, :] < cache_lengths[:, None]
    score_scale = (DK + RR) ** (-0.5)
    outputs = []
    for step_index in range(step_count):
        fresh_valid = jnp.arange(step_count, dtype=jnp.int32) <= step_index
        valid = jnp.concatenate([prompt_valid, jnp.broadcast_to(fresh_valid[None, :], (batch, step_count))], axis=1)
        query_now = query_all[step_index].reshape(batch, heads, width)
        scores = jnp.einsum('bhc,blc->bhl', query_now.astype(jnp.float32), keys_all.astype(jnp.float32)) * score_scale
        scores = jnp.where(valid[:, None, :], scores, -1e+30)
        top_score = lax.optimization_barrier(jnp.max(scores, axis=-1, keepdims=True))
        raised = jnp.exp(scores - top_score)
        weights = (raised / lax.optimization_barrier(jnp.sum(raised, axis=-1, keepdims=True))).astype(jnp.bfloat16)
        context = jnp.einsum('bhl,blr->bhr', weights.astype(jnp.float32), keys_all[..., :rank].astype(jnp.float32)).astype(jnp.bfloat16)
        result = jnp.einsum('bhr,hrv->bhv', context.astype(jnp.float32), up_value.astype(jnp.float32))
        outputs.append(result.reshape(batch, heads * value_dim).astype(jnp.bfloat16))
    return jnp.stack(outputs)

def sample_prompts(sample_counts):
    sample_ids = jnp.arange(SAMPLES, dtype=jnp.int32)
    decoder = sample_ids // S_DEV
    offset = sample_ids % S_DEV
    owner = (decoder + offset) % OWNERS
    bounds = jnp.cumsum(sample_counts, axis=1).astype(jnp.int32)[owner]
    local = lax.optimization_barrier(jnp.sum((bounds <= offset[:, None]).astype(jnp.int32), axis=1))
    return (owner * P_DEV + local).astype(jnp.int32)

def reference(kda_prefill, latent_prefill, prompt_len, sample_counts, kda_q, kda_k, kda_v, kda_decay, kda_beta, mla_q, mla_new, w_uv):
    prompts = sample_prompts(sample_counts)
    blocks = SAMPLES // S_DEV

    def split_blocks(values):
        shaped = values.reshape((STEPS, blocks, S_DEV) + values.shape[2:])
        return jnp.swapaxes(shaped, 0, 1)

    def per_block(inputs):
        block_ids, query_b, key_b, value_b, decay_b, beta_b, latq_b, fresh_b = inputs
        start_state = kda_prefill[block_ids].astype(jnp.float32)
        delta_out = delta_run(start_state, query_b, key_b, value_b, decay_b, beta_b)
        latent_out = latent_run(latent_prefill[block_ids], prompt_len[block_ids], latq_b, fresh_b, w_uv)
        return (delta_out, latent_out)
    delta_all, latent_all = lax.map(per_block, (prompts.reshape(blocks, S_DEV), split_blocks(kda_q), split_blocks(kda_k), split_blocks(kda_v), split_blocks(kda_decay), split_blocks(kda_beta), split_blocks(mla_q), split_blocks(mla_new)))
    kda_out = jnp.swapaxes(delta_all, 0, 1).reshape(STEPS, SAMPLES, H * DV)
    mla_out = jnp.swapaxes(latent_all, 0, 1).reshape(STEPS, SAMPLES, H * DV)
    return (kda_out, mla_out)
```

```python
import functools

import jax
import jax.numpy as jnp
from jax import lax
from jax.experimental import pallas as pl
from jax.experimental.pallas import tpu as pltpu
from jax.sharding import PartitionSpec as P

F32 = jnp.float32
BF16 = jnp.bfloat16
NEG = -1e30


def split(x, n):
    if n & (n - 1) == 0:
        return lax.shift_right_logical(x, jnp.full_like(x, n.bit_length() - 1)), x & (n - 1)
    return lax.div(x, jnp.full_like(x, n)), lax.rem(x, jnp.full_like(x, n))


def wrap(x, n):
    return jnp.where(x < 0, x + n, x)


def lanes(shape, dim):
    return lax.broadcasted_iota(jnp.int32, shape, dim)


def prompt_at(counts_ref, owner, j):
    bound = jnp.int32(0)
    k = jnp.zeros_like(j)
    for i in range(counts_ref.shape[1]):
        bound = bound + counts_ref[owner, i]
        k = k + (bound <= j).astype(jnp.int32)
    return k


def fan_slot(row, me, group, slots, steps):
    other, rest = split(row, slots * steps)
    slot, step = split(rest, steps)
    return other, slot, step


def plane_slot(row, carry_of, cols, pairs, steps, per_shift):
    shift, rest = split(row, per_shift)
    hop, rest = split(rest, pairs * steps)
    pair, step = split(rest, steps)
    i = wrap(hop - carry_of(shift), cols["depth"]) + cols["depth"] * pair
    return step, i, shift + cols["width"] * i


def dot(a, b):
    return lax.dot_general(a, b, (((1,), (0,)), ((), ())), preferred_element_type=F32)


def dot_t(a, b):
    return lax.dot_general(a, b, (((1,), (1,)), ((), ())), preferred_element_type=F32)


def reads_kernel(geo, q_ref, k_ref, g_ref, b_ref, r_ref, a_ref, raw):
    steps, per, width = q_ref.shape
    heads = b_ref.shape[2]
    dk = width // heads
    me = lax.axis_index("roll")
    coef = [[] for _ in range(steps * (steps + 1) // 2)]
    for h in range(heads):
        sl = slice(h * dk, (h + 1) * dk)
        qs, ks, ds, bs = [], [], [], []
        for t in range(steps):
            q = q_ref[t, :, sl].astype(F32)
            k = k_ref[t, :, sl].astype(F32)
            qs.append(q * lax.rsqrt(jnp.sum(q * q, axis=1, keepdims=True) + 1e-06))
            ks.append(k * lax.rsqrt(jnp.sum(k * k, axis=1, keepdims=True) + 1e-06))
            ds.append(jnp.exp(-g_ref[t, :, sl]))
            bs.append(b_ref[t, :, h : h + 1])
        n = 0
        for t in range(steps):
            u = qs[t]
            for i in range(t, -1, -1):
                a = bs[i] * jnp.sum(ks[i] * u, axis=1, keepdims=True)
                u = ds[i] * (u - a * ks[i])
                coef[n].append(a)
                n += 1
            raw[t * per : (t + 1) * per, sl] = u.astype(BF16)
    for n, c in enumerate(coef):
        a_ref[n] = jnp.concatenate(c, axis=1)
    rows = r_ref.shape[0]
    group, slots = geo["group"], geo["slots"]
    row, col = lanes((rows, steps * per), 0), lanes((rows, steps * per), 1)
    other, slot, step = fan_slot(row, me, group, slots, steps)
    j = wrap(other - me, group) + group * slot
    pick = ((col == step * per + j) & (j < per)).astype(F32).astype(BF16)
    r_ref[...] = dot(pick, raw[...]).astype(BF16)


def state_kernel(geo, counts_ref, r_ref, s_ref, y_ref):
    rows = r_ref.shape[0]
    prompts, heads, dk, dv = s_ref.shape
    me = lax.axis_index("roll")
    group, slots, steps = geo["group"], geo["slots"], geo["steps"]
    row = lanes((rows, dk), 0)
    other, slot, step = fan_slot(row, me, group, slots, steps)
    j = wrap(me - other, group) + group * slot
    k = prompt_at(counts_ref, me, j)
    keep = [(k == p).astype(F32).astype(BF16) for p in range(prompts)]
    for h in range(heads):
        r = r_ref[:, h * dk : (h + 1) * dk]
        acc = dot(r * keep[0], s_ref[0, h])
        for p in range(1, prompts):
            acc = acc + dot(r * keep[p], s_ref[p, h])
        y_ref[:, h * dv : (h + 1) * dv] = acc.astype(BF16)


def kda_out_kernel(geo, y_ref, a_ref, v_ref, o_ref):
    steps, per, width = v_ref.shape
    heads = a_ref.shape[2]
    dv = width // heads
    rows = y_ref.shape[0]
    me = lax.axis_index("roll")
    group, slots = geo["group"], geo["slots"]
    row, col = lanes((steps * per, rows), 0), lanes((steps * per, rows), 1)
    other, slot, step = fan_slot(col, me, group, slots, steps)
    j = wrap(other - me, group) + group * slot
    pick = ((row == step * per + j) & (j < per)).astype(F32).astype(BF16)
    for h in range(heads):
        sl = slice(h * dv, (h + 1) * dv)
        y = dot(pick, y_ref[:, sl])
        n = 0
        for t in range(steps):
            out = y[t * per : (t + 1) * per]
            for i in range(t, -1, -1):
                out = out + a_ref[n, :, h : h + 1] * v_ref[i, :, sl].astype(F32)
                n += 1
            o_ref[t, :, sl] = out.astype(BF16)


def send_pick(geo, shape, row_dim, b):
    row, col = lanes(shape, row_dim), lanes(shape, 1 - row_dim)
    width = geo["width"]

    def carry(shift):
        return (b + shift >= width).astype(jnp.int32)

    step, i, j = plane_slot(row, carry, geo, geo["pairs"], geo["steps"], geo["per_shift"])
    hit = (col == step * geo["per"] + j) & (i < geo["per"] // width)
    return hit.astype(F32).astype(BF16)


def send_kernel(geo, q_ref, f_ref, *o_refs):
    total, wide = q_ref.shape
    fresh = f_ref.shape[1]
    me = lax.axis_index("roll")
    _, b = split(me, geo["width"])
    n = geo["per_shift"]
    pick = send_pick(geo, (n * geo["width"], total), 0, b)
    step = geo["chunk"]
    for at in range(0, wide, step):
        out = dot(pick, q_ref[:, at : at + step]).astype(BF16)
        for s, o_ref in enumerate(o_refs):
            o_ref[:, at : at + step] = out[s * n : (s + 1) * n]
    out = dot(pick, f_ref[...]).astype(BF16)
    for s, o_ref in enumerate(o_refs):
        o_ref[:, wide : wide + fresh] = out[s * n : (s + 1) * n]
        o_ref[:, wide + fresh :] = jnp.zeros((n, o_ref.shape[1] - wide - fresh), BF16)


def latent_kernel(geo, counts_ref, len_ref, w_ref, *refs):
    width, hops, pairs, steps = geo["width"], geo["hops"], geo["pairs"], geo["steps"]
    depth, halves, cache, prompts = geo["depth"], geo["halves"], geo["cache"], geo["prompts"]
    n, tile = geo["per_shift"], geo["tile"]
    q_refs, refs = refs[:width], refs[width:]
    k_refs, refs = refs[:halves], refs[halves:]
    o_refs, (qp, k_even, k_odd, ctx) = refs[:width], refs[width:]
    heads, rank, dv = w_ref.shape
    wide = o_refs[0].shape[1] // dv * geo["entry"]
    entry, padded = geo["entry"], k_even.shape[1]
    me = lax.axis_index("roll")
    half = lax.axis_index("exp")
    a, b = split(me, width)
    rows = n * width
    row, col = lanes((rows, rows), 0), lanes((rows, rows), 1)
    hop, rest = split(row, tile)
    shift, rest = split(rest, pairs * steps)
    regroup = (col == shift * n + hop * (pairs * steps) + rest).astype(F32).astype(BF16)
    shift2, rest2 = split(row, n)
    hop2, rest2 = split(rest2, pairs * steps)
    back = (col == hop2 * tile + shift2 * (pairs * steps) + rest2).astype(F32).astype(BF16)
    step = geo["chunk"]
    total = q_refs[0].shape[1]
    for at in range(0, total, step):
        to = min(at + step, total)
        part = jnp.concatenate([q[:, at:to] for q in q_refs], axis=0)
        qp[:, at:to] = dot(regroup, part).astype(BF16)
    per_half = prompts * cache // halves
    local = cache // halves
    keys = prompts * cache
    cols = k_even.shape[0]
    k_even[:, entry:] = jnp.zeros((cols, padded - entry), BF16)
    k_even[keys:, :] = jnp.zeros((cols - keys, padded), BF16)
    scale = geo["scale"]
    half_heads = heads // 2
    for hop in range(hops):
        owner_a = a + hop
        owner = jnp.where(owner_a >= depth, owner_a - depth, owner_a) * width + b
        for e in range(halves):
            k_even[e * per_half : (e + 1) * per_half, :entry] = k_refs[e][
                hop * per_half : (hop + 1) * per_half, :
            ]
        k_even[keys : keys + tile, :] = qp[hop * tile : (hop + 1) * tile, wide : wide + padded]
        k_odd[...] = pltpu.roll(k_even[...].astype(F32), padded - entry, 1).astype(BF16)
        r0 = lanes((tile, cols), 0)
        c0 = lanes((tile, cols), 1)
        shift, rest = split(r0, pairs * steps)
        pair, step_r = split(rest, steps)
        carry = (shift > b).astype(jnp.int32)
        i = wrap(hop - carry, depth) + depth * pair
        k = prompt_at(counts_ref, owner, shift + width * i)
        e, rest = split(c0, per_half)
        kk, pos = split(rest, local)
        e = e + half
        pos = jnp.where(e >= halves, e - halves, e) * local + pos
        length = jnp.zeros_like(pos)
        for p in range(prompts):
            length = jnp.where(kk == p, len_ref[owner * prompts + p], length)
        in_prompt = (c0 < keys) & (kk == k) & (pos < length)
        behind = r0 - (c0 - keys)
        in_fresh = (c0 >= keys) & (behind >= 0) & (behind <= step_r)
        allowed = (in_prompt | in_fresh)[None]
        parts = []
        for odd, k_ref in enumerate((k_even, k_odd)):
            starts = [2 * entry * p + odd * (2 * entry - padded) for p in range(half_heads)]
            query = jnp.concatenate(
                [qp[hop * tile : (hop + 1) * tile, s : s + padded] for s in starts], axis=0
            )
            scores = dot_t(query, k_ref[...]).reshape(half_heads, tile, cols) * scale
            scores = jnp.where(allowed, scores, NEG)
            top = jnp.max(scores, axis=-1, keepdims=True)
            raised = jnp.exp(scores - top)
            weights = raised / jnp.sum(raised, axis=-1, keepdims=True)
            parts.append(weights.reshape(half_heads * tile, cols).astype(BF16))
        weights = jnp.concatenate(parts, axis=0)
        context = dot(weights, k_even[:, :rank]).astype(BF16)
        for at in range(heads):
            ctx[at, hop * tile : (hop + 1) * tile, :] = context[at * tile : (at + 1) * tile]
    for h in range(heads):
        at = (h % 2) * half_heads + h // 2
        out = dot(ctx[at], w_ref[h]).astype(BF16)
        out = dot(back, out).astype(BF16)
        for s, o_ref in enumerate(o_refs):
            o_ref[:, h * dv : (h + 1) * dv] = out[s * n : (s + 1) * n]


def mla_out_kernel(geo, *refs):
    refs, o_ref = refs[:-1], refs[-1]
    me = lax.axis_index("roll")
    _, b = split(me, geo["width"])
    n = geo["per_shift"]
    total, wide = o_ref.shape
    pick = send_pick(geo, (total, n * geo["width"]), 1, b)
    step = geo["chunk"]
    for at in range(0, wide, step):
        part = jnp.concatenate([r[:, at : at + step] for r in refs], axis=0)
        o_ref[:, at : at + step] = dot(pick, part).astype(BF16)


def call(kernel, geo, out, args, smem=0, scratch=()):
    spaces = [pltpu.SMEM] * smem + [pltpu.VMEM] * (len(args) - smem)
    return pl.pallas_call(
        functools.partial(kernel, geo),
        out_shape=out,
        in_specs=[pl.BlockSpec(memory_space=s) for s in spaces],
        scratch_shapes=list(scratch),
        compiler_params=pltpu.CompilerParams(vmem_limit_bytes=48 * 1024 * 1024),
        name=kernel.__name__,
    )(*args)


def pad_to(n, m):
    return -(-n // m) * m


def on_device(
    kda_prefill,
    latent_prefill,
    prompt_len,
    sample_counts,
    kda_q,
    kda_k,
    kda_v,
    kda_decay,
    kda_beta,
    mla_q,
    mla_new,
    w_uv,
):
    group = lax.axis_size("roll")
    halves = lax.axis_size("exp")
    steps, per, kda_width = kda_q.shape
    heads = kda_beta.shape[2]
    prompts, local, entry = latent_prefill.shape
    cache = local * halves
    _, rank, dv = w_uv.shape
    width = 4
    depth = group // width
    slots = -(-per // group)
    per_mate = per // width
    hops = min(depth, per_mate + 1)
    pairs = max(-(-per_mate // depth), -(-16 // (width * steps)))
    padded = pad_to(entry, 128)
    geo = dict(
        group=group,
        halves=halves,
        steps=steps,
        per=per,
        width=width,
        depth=depth,
        slots=slots,
        hops=hops,
        pairs=pairs,
        prompts=prompts,
        cache=cache,
        entry=entry,
        per_shift=hops * pairs * steps,
        tile=width * pairs * steps,
        scale=192.0**-0.5,
        chunk=1152,
    )
    shape = jax.ShapeDtypeStruct

    def mates(sign, s):
        return [(i, i // width * width + (i + sign * s) % width) for i in range(group)]

    coefs = steps * (steps + 1) // 2
    reads, coef = call(
        reads_kernel,
        geo,
        (shape((group * slots * steps, kda_width), BF16), shape((coefs, per, heads), F32)),
        (kda_q, kda_k, kda_decay, kda_beta),
        scratch=[pltpu.VMEM((steps * per, kda_width), BF16)],
    )
    got = lax.all_to_all(reads, "roll", 0, 0, tiled=True)

    own = latent_prefill.reshape(prompts * local, entry)
    column = [own] + [
        lax.ppermute(own, "roll", [(i, (i - width * h) % group) for i in range(group)])
        for h in range(1, hops)
    ]
    column = jnp.concatenate(column, axis=0)
    caches = [column] + [
        lax.ppermute(column, "exp", [(i, (i - e) % halves) for i in range(halves)])
        for e in range(1, halves)
    ]
    wide = mla_q.shape[2]
    parcels = call(
        send_kernel,
        geo,
        tuple(shape((geo["per_shift"], wide + padded), BF16) for _ in range(width)),
        (mla_q.reshape(steps * per, wide), mla_new.reshape(steps * per, entry)),
    )
    queries = [parcels[0]] + [
        lax.ppermute(parcels[s], "roll", mates(1, s)) for s in range(1, width)
    ]
    products = call(
        state_kernel,
        geo,
        shape((group * slots * steps, kda_width), BF16),
        (sample_counts, got, kda_prefill),
        smem=1,
    )
    back = lax.all_to_all(products, "roll", 0, 0, tiled=True)
    cols = pad_to(prompts * cache + geo["tile"], 128)
    results = call(
        latent_kernel,
        geo,
        tuple(shape((geo["per_shift"], heads * dv), BF16) for _ in range(width)),
        (sample_counts, prompt_len, w_uv, *queries, *caches),
        smem=2,
        scratch=[
            pltpu.VMEM((geo["per_shift"] * width, wide + padded), BF16),
            pltpu.VMEM((cols, padded), BF16),
            pltpu.VMEM((cols, padded), BF16),
            pltpu.VMEM((heads, hops * geo["tile"], rank), BF16),
        ],
    )
    returned = [results[0]] + [
        lax.ppermute(results[s], "roll", mates(-1, s)) for s in range(1, width)
    ]
    mla_out = call(mla_out_kernel, geo, shape((steps * per, heads * dv), BF16), returned)
    kda_out = call(
        kda_out_kernel, geo, shape((steps, per, kda_width), BF16), (back, coef, kda_v)
    )
    return (kda_out, mla_out.reshape(steps, per, heads * dv))


def solution(mesh):
    return jax.shard_map(
        on_device,
        mesh=mesh,
        in_specs=(
            P("roll", "exp", None, None),
            P("roll", "exp", None),
            P(),
            P(),
            P(None, "roll", "exp"),
            P(None, "roll", "exp"),
            P(None, "roll", "exp"),
            P(None, "roll", "exp"),
            P(None, "roll", "exp"),
            P(None, "roll", "exp"),
            P(None, "roll", None),
            P("exp", None, None),
        ),
        out_specs=(P(None, "roll", "exp"), P(None, "roll", "exp")),
        check_vma=False,
    )
```

```python
import functools

import jax
import jax.numpy as jnp
from jax import lax
from jax.experimental import pallas as pl
from jax.experimental.pallas import tpu as pltpu
from jax.sharding import PartitionSpec as P

F32 = jnp.float32
BF16 = jnp.bfloat16
NEG = -1e30


def split(x, n):
    if n & (n - 1) == 0:
        return lax.shift_right_logical(x, jnp.full_like(x, n.bit_length() - 1)), x & (n - 1)
    return lax.div(x, jnp.full_like(x, n)), lax.rem(x, jnp.full_like(x, n))


def wrap(x, n):
    return jnp.where(x < 0, x + n, x)


def lanes(shape, dim):
    return lax.broadcasted_iota(jnp.int32, shape, dim)


def prompt_at(counts_ref, owner, j):
    bound = jnp.int32(0)
    k = jnp.zeros_like(j)
    for i in range(counts_ref.shape[0]):
        bound = bound + counts_ref[i, owner]
        k = k + (bound <= j).astype(jnp.int32)
    return k


def fan_rows(geo, shape, dim, me):
    group, slots, steps, parts, per = (geo[n] for n in ("group", "slots", "steps", "parts", "per"))
    other, rest = split(lanes(shape, dim), parts * slots * steps)
    part, rest = split(rest, slots * steps)
    slot, step = split(rest, steps)
    j = wrap(other - me, group) + group * slot
    return part, jnp.where(j < per, step * per + j, -1)


def one_hot(hit):
    return hit.astype(F32).astype(BF16)


def dot(a, b):
    return lax.dot_general(a, b, (((1,), (0,)), ((), ())), preferred_element_type=F32)


def dot_first(a, b):
    return lax.dot_general(a, b, (((0,), (0,)), ((), ())), preferred_element_type=F32)


def dot_t(a, b):
    return lax.dot_general(a, b, (((1,), (1,)), ((), ())), preferred_element_type=F32)


def row_sums(x, ones):
    return dot(x.astype(BF16), ones)


def reads_kernel(geo, q_hbm, k_hbm, g_hbm, b_hbm, r_ref, a_ref, q_ref, k_ref, g_ref, b_ref, raw, sems):
    _, per, width = q_ref.shape
    heads = geo["heads"]
    dk = width // heads
    parts = geo["parts"]
    wide = width // parts
    beta_copy = pltpu.make_async_copy(b_hbm, b_ref, sems.at[parts, 0])
    beta_copy.start()
    copies = []
    for c in range(parts):
        sl = pl.ds(c * wide, wide)
        for n, (src, dst) in enumerate(((q_hbm, q_ref), (k_hbm, k_ref), (g_hbm, g_ref))):
            copies.append(pltpu.make_async_copy(src.at[:, :, sl], dst.at[:, :, sl], sems.at[c, n]))
            copies[-1].start()
    me = lax.axis_index("roll")
    unit = 2 * dk
    ones = one_hot(split(lanes((unit, unit), 0), dk)[0] == split(lanes((unit, unit), 1), dk)[0])
    rows, rows_in = r_ref.shape[0], raw.shape[0]
    part, place = fan_rows(geo, (rows, rows_in), 0, me)
    pick = one_hot((lanes((rows, rows_in), 1) == part * (2 * per) + place) & (place >= 0))
    lane = lanes((per, a_ref.shape[2]), 1)
    coef = [jnp.zeros((per, a_ref.shape[2]), F32) for _ in range(3)]
    spread = one_hot(lanes((heads, width), 0) == split(lanes((heads, width), 1), dk)[0])
    betas = []
    beta_copy.wait()
    for t in range(2):
        beta = b_ref[t]
        high = beta.astype(BF16)
        low = (beta - high.astype(F32)).astype(BF16)
        betas.append(dot_first(high, spread) + dot_first(low, spread))
    for c in range(parts):
        for copy in copies[3 * c : 3 * c + 3]:
            copy.wait()
        for at in range(c * wide, (c + 1) * wide, unit):
            sl = slice(at, at + unit)
            q1, q2 = q_ref[0, :, sl].astype(F32), q_ref[1, :, sl].astype(F32)
            k1, k2 = k_ref[0, :, sl].astype(F32), k_ref[1, :, sl].astype(F32)
            d1, d2 = jnp.exp(-g_ref[0, :, sl]), jnp.exp(-g_ref[1, :, sl])
            h = at // dk

            dq2, dk2 = d2 * q2, d2 * k2
            terms = (q1 * q1, k1 * k1, q2 * q2, k2 * k2, k1 * q1, k2 * q2, k1 * dq2, k1 * dk2)
            sums = row_sums(jnp.concatenate(terms, axis=0), ones)
            s = [sums[n * per : (n + 1) * per] for n in range(8)]
            rq1, rk1, rq2, rk2 = (lax.rsqrt(x + 1e-06) for x in s[:4])
            b1, b2 = betas[0][:, sl], betas[1][:, sl]
            a11 = b1 * (s[4] * rk1 * rq1)
            a22 = b2 * (s[5] * rk2 * rq2)
            a22k = a22 * rk2
            a21 = b1 * (rk1 * (rq2 * s[6] - a22k * s[7]))
            r1 = d1 * (rq1 * q1 - (a11 * rk1) * k1)
            r2 = d1 * (rq2 * dq2 - a22k * dk2 - (a21 * rk1) * k1)
            to = slice(at - c * wide, at - c * wide + unit)
            raw[2 * c * per : (2 * c + 1) * per, to] = r1.astype(BF16)
            raw[(2 * c + 1) * per : (2 * c + 2) * per, to] = r2.astype(BF16)
            for n, a in enumerate((a11, a22, a21)):
                for m in range(2):
                    coef[n] = jnp.where(lane == h + m, a[:, m * dk : (m + 1) * dk], coef[n])
    for n in range(3):
        a_ref[n] = coef[n]
    r_ref[...] = dot(pick, raw[...]).astype(BF16)


def state_kernel(geo, s_hbm, c_hbm, *refs):
    r_ref, y_ref, s_ref, r_all, y_all, counts_ref, sems = refs[-7:]
    rows, wide = r_ref.shape
    prompts, heads, dk, dv = s_ref.shape
    me = lax.axis_index("roll")
    group, slots, steps, parts = geo["group"], geo["slots"], geo["steps"], geo["parts"]
    copies = [pltpu.make_async_copy(c_hbm, counts_ref, sems.at[parts])]
    for c in range(parts):
        sl = pl.ds(c * (heads // parts), heads // parts)
        copies.append(pltpu.make_async_copy(s_hbm.at[:, sl], s_ref.at[:, sl], sems.at[c]))
    for copy in copies:
        copy.start()
    few, own = rows // parts, slots * steps
    part, rest = split(lanes((rows, rows), 0), few)
    other, rest = split(rest, own)
    sort = one_hot(lanes((rows, rows), 1) == (other * parts + part) * own + rest)
    part, rest = split(lanes((rows, rows), 1), few)
    other, rest = split(rest, own)
    back = one_hot(lanes((rows, rows), 0) == (other * parts + part) * own + rest)
    r_all[...] = dot(sort, r_ref[...]).astype(BF16)
    copies[0].wait()
    other, rest = split(lanes((few, dk), 0), own)
    j = wrap(me - other, group) + group * split(rest, steps)[0]
    k = prompt_at(counts_ref, me, j)
    keep = [one_hot(k == p) for p in range(prompts)]
    for c in range(parts):
        copies[1 + c].wait()
        for at in range(wide // dk):
            h = c * (wide // dk) + at
            r = r_all[c * few : (c + 1) * few, at * dk : (at + 1) * dk]
            acc = dot(r * keep[0], s_ref[0, h])
            for p in range(1, prompts):
                acc = acc + dot(r * keep[p], s_ref[p, h])
            y_all[c * few : (c + 1) * few, at * dv : (at + 1) * dv] = acc.astype(BF16)
    y_ref[...] = dot(back, y_all[...]).astype(BF16)


def kda_out_kernel(geo, v_hbm, _, y_ref, a_ref, o_ref, v_ref, sem):
    copy = pltpu.make_async_copy(v_hbm, v_ref, sem)
    copy.start()
    _, per, width = v_ref.shape
    rows, wide = y_ref.shape
    heads = geo["heads"]
    dv = width // heads
    me = lax.axis_index("roll")
    parts = geo["parts"]
    shape = (2 * per * parts, rows)
    part, place = fan_rows(geo, shape, 1, me)
    pick = one_hot((lanes(shape, 0) == part * (2 * per) + place) & (place >= 0))
    y_all = dot(pick, y_ref[...])
    copy.wait()
    for c in range(parts):
        y = y_all[c * 2 * per : (c + 1) * 2 * per]
        for at in range(wide // dv):
            h = c * (wide // dv) + at
            sl = slice(h * dv, (h + 1) * dv)
            v1, v2 = v_ref[0, :, sl].astype(F32), v_ref[1, :, sl].astype(F32)
            a11, a22, a21 = (a_ref[n, :, h : h + 1] for n in range(3))
            here = y[:, at * dv : (at + 1) * dv]
            o_ref[0, :, sl] = (here[:per] + a11 * v1).astype(BF16)
            o_ref[1, :, sl] = (here[per:] + a21 * v1 + a22 * v2).astype(BF16)


def select_kernel(geo, c_hbm, *refs):
    width, depth, hops, prompts, per_mate = (
        geo[n] for n in ("width", "depth", "hops", "prompts", "per_mate")
    )
    refs, (pool, counts_ref, sem) = refs[1:-3], refs[-3:]
    pieces, o_refs = refs[:hops], refs[hops:]
    copy = pltpu.make_async_copy(c_hbm, counts_ref, sem)
    copy.start()
    _, local, padded = pool.shape
    entry = geo["entry"]
    pool[:, :, entry:] = jnp.zeros((hops * prompts, local, padded - entry), BF16)
    for h, piece in enumerate(pieces):
        pool[h * prompts : (h + 1) * prompts, :, :entry] = piece[...]
    copy.wait()
    a, b = split(lax.axis_index("roll"), width)
    for s, o_ref in enumerate(o_refs):
        carry = (b < s).astype(jnp.int32)
        for i in range(per_mate):
            hop = wrap(i + carry - i // depth * depth - depth, depth)
            owner = wrap(a + hop - depth, depth) * width + b
            k = prompt_at(counts_ref, owner, jnp.int32(s + width * i))
            o_ref[i * local : (i + 1) * local, :] = pool[hop * prompts + k]


def query_kernel(geo, q_hbm, f_hbm, _, o_ref, n_ref, q_ref, f_ref, sems):
    total, wide = q_ref.shape
    width, per, steps, entry = geo["width"], geo["per"], geo["steps"], geo["entry"]
    padded = o_ref.shape[1]
    heads = wide // entry
    unit = 2 * entry
    n = total // width
    fresh_copy = pltpu.make_async_copy(f_hbm, f_ref, sems.at[heads // 2])
    fresh_copy.start()
    copies = []
    for c in range(heads // 2):
        sl = pl.ds(c * unit, unit)
        copies.append(pltpu.make_async_copy(q_hbm.at[:, sl], q_ref.at[:, sl], sems.at[c]))
        copies[-1].start()
    row, col = lanes((total, total), 0), lanes((total, total), 1)
    shift, rest = split(row, n)
    i, step = split(rest, steps)
    pick = one_hot(col == step * per + shift + width * i)
    fresh_copy.wait()
    n_ref[:, :entry] = dot(pick, f_ref[...]).astype(BF16)
    n_ref[:, entry:] = jnp.zeros((total, padded - entry), BF16)
    for c, copy in enumerate(copies):
        copy.wait()
        out = dot(pick, q_ref[:, c * unit : (c + 1) * unit])
        even = out[:, :padded].astype(BF16)
        odd = pltpu.roll(out[:, unit - padded :], entry, 1).astype(BF16)
        for s in range(width):
            at = (s * heads + 2 * c) * n
            o_ref[at : at + n, :] = even[s * n : (s + 1) * n]
            o_ref[at + n : at + 2 * n, :] = odd[s * n : (s + 1) * n]


def latent_kernel(geo, w_hbm, c_hbm, l_hbm, _, q_ref, n_ref, *refs):
    width, steps, per, group = geo["width"], geo["steps"], geo["per"], geo["group"]
    halves, cache, prompts, per_mate = (
        geo[n] for n in ("halves", "cache", "prompts", "per_mate")
    )
    k_refs = refs[: width * halves]
    o_ref, keys, ctx, out, w_ref, counts_ref, len_ref, sems = refs[width * halves :]
    copies = [
        pltpu.make_async_copy(src, dst, sems.at[n])
        for n, (src, dst) in enumerate(((c_hbm, counts_ref), (l_hbm, len_ref), (w_hbm, w_ref)))
    ]
    for copy in copies:
        copy.start()
    heads, rank, dv = w_ref.shape
    me = lax.axis_index("roll")
    half = lax.axis_index("exp")
    local = cache // halves
    piece = per_mate * local
    total = per_mate * cache
    n = per_mate * steps
    cols = keys.shape[0]
    keys[total + n :, :] = jnp.zeros((cols - total - n, keys.shape[1]), BF16)
    row, col = lanes((n, cols), 0), lanes((n, cols), 1)
    sample, step = split(row, steps)
    e, rest = split(col, piece)
    other, pos = split(rest, local)
    e = e + half
    pos = jnp.where(e >= halves, e - halves, e) * local + pos
    pos = jnp.where((col < total) & (other == sample), pos, cache)
    behind = row - (col - total)
    in_fresh = (col >= total) & (behind >= 0) & (behind <= step)
    copies[0].wait()
    copies[1].wait()
    for s in range(width):
        length = jnp.zeros_like(pos)
        for i in range(per_mate):
            j = s + width * i
            owner = split(me + j, group)[1]
            k = prompt_at(counts_ref, owner, jnp.int32(j))
            length = jnp.where(sample == i, len_ref[owner * prompts + k], length)
        allowed = ((pos < length) | in_fresh)[None]
        for e in range(halves):
            keys[e * piece : (e + 1) * piece, :] = k_refs[s * halves + e][...]
        keys[total : total + n, :] = n_ref[s * n : (s + 1) * n, :]
        query = q_ref[s * heads * n : (s + 1) * heads * n, :]
        scores = dot_t(query, keys[...]).reshape(heads, n, cols) * geo["scale"]
        scores = jnp.where(allowed, scores, NEG)
        top = jnp.max(scores, axis=-1, keepdims=True)
        raised = jnp.exp(scores - top)
        weights = raised / jnp.sum(raised, axis=-1, keepdims=True)
        weights = weights.reshape(heads * n, cols).astype(BF16)
        context = dot(weights, keys[:, :rank]).astype(BF16)
        for h in range(heads):
            ctx[h, s * n : (s + 1) * n, :] = context[h * n : (h + 1) * n]
    copies[2].wait()
    for h in range(heads):
        out[:, h * dv : (h + 1) * dv] = dot(ctx[h], w_ref[h]).astype(BF16)
    rows = steps * per
    shift, rest = split(lanes((rows, rows), 1), n)
    sample, step = split(rest, steps)
    place = step * per + shift + width * sample
    pick = one_hot(lanes((rows, rows), 0) == place)
    o_ref[...] = dot(pick, out[...]).astype(BF16)


def cost(us):
    return pl.CostEstimate(
        flops=2_000_000_000 * us, bytes_accessed=3_000_000 * us, transcendentals=20_000_000 * us
    )


def call(kernel, geo, out, args, hbm=0, after=0, scratch=(), mib=16, us=0):
    spaces = [pltpu.HBM] * hbm + [pl.ANY] * after + [pltpu.VMEM] * (len(args) - hbm - after)
    args = [
        pltpu.with_memory_space_constraint(x, pltpu.HBM) if s == pltpu.HBM else x
        for x, s in zip(args, spaces, strict=True)
    ]
    return pl.pallas_call(
        functools.partial(kernel, geo),
        out_shape=out,
        in_specs=[pl.BlockSpec(memory_space=s) for s in spaces],
        scratch_shapes=list(scratch),
        cost_estimate=cost(us),
        compiler_params=pltpu.CompilerParams(vmem_limit_bytes=mib * 1024 * 1024),
        name=kernel.__name__,
    )(*args)


def hold(x, first):
    return pl.pallas_call(
        lambda *refs: None,
        out_shape=tuple(jax.ShapeDtypeStruct(a.shape, a.dtype) for a in x),
        in_specs=[pl.BlockSpec(memory_space=pl.ANY)] * (len(x) + 1),
        out_specs=[pl.BlockSpec(memory_space=pl.ANY)] * len(x),
        input_output_aliases={n + 1: n for n in range(len(x))},
        cost_estimate=cost(20),
        name="hold",
    )(first, *x)


def pad_to(n, m):
    return -(-n // m) * m


def on_device(
    kda_prefill,
    latent_prefill,
    prompt_len,
    sample_counts,
    kda_q,
    kda_k,
    kda_v,
    kda_decay,
    kda_beta,
    mla_q,
    mla_new,
    w_uv,
):
    group = lax.axis_size("roll")
    halves = lax.axis_size("exp")
    steps, per, kda_width = kda_q.shape
    heads = kda_beta.shape[2]
    prompts, local, entry = latent_prefill.shape
    cache = local * halves
    _, rank, dv = w_uv.shape
    width = 4
    depth = group // width
    slots = -(-per // group)
    per_mate = per // width
    hops = min(depth, per_mate + 1)
    padded = pad_to(entry, 128)
    parts = max(1, min(16 // (slots * steps), heads // 2))
    geo = dict(
        group=group,
        halves=halves,
        steps=steps,
        per=per,
        width=width,
        depth=depth,
        slots=slots,
        hops=hops,
        prompts=prompts,
        cache=cache,
        entry=entry,
        per_mate=per_mate,
        scale=192.0**-0.5,
        heads=heads,
        parts=parts,
    )
    shape = jax.ShapeDtypeStruct

    def mates(sign, s):
        return [(i, i // width * width + (i + sign * s) % width) for i in range(group)]

    counts = sample_counts.T
    fan = (group * parts * slots * steps, kda_width // parts)
    reads, coef = call(
        reads_kernel,
        geo,
        (shape(fan, BF16), shape((3, per, 128), F32)),
        (kda_q, kda_k, kda_decay, jnp.swapaxes(kda_beta, 1, 2)),
        hbm=4,
        scratch=[
            pltpu.VMEM(kda_q.shape, BF16),
            pltpu.VMEM(kda_q.shape, BF16),
            pltpu.VMEM(kda_q.shape, F32),
            pltpu.VMEM((steps, heads, per), F32),
            pltpu.VMEM((steps * per * parts, kda_width // parts), BF16),
            pltpu.SemaphoreType.DMA((parts + 1, 3)),
        ],
    )
    got = lax.all_to_all(reads, "roll", 0, 0, tiled=True)

    column = [latent_prefill] + [
        lax.ppermute(latent_prefill, "roll", [(i, (i - width * h) % group) for i in range(group)])
        for h in range(1, hops)
    ]
    wide = mla_q.shape[2]
    rows = steps * per
    queries, fresh = call(
        query_kernel,
        geo,
        (shape((heads * rows, padded), BF16), shape((rows, padded), BF16)),
        (mla_q.reshape(rows, wide), mla_new.reshape(rows, entry), reads),
        hbm=2,
        after=1,
        scratch=[
            pltpu.VMEM((rows, wide), BF16),
            pltpu.VMEM((rows, entry), BF16),
            pltpu.SemaphoreType.DMA((heads // 2 + 1,)),
        ],
    )
    chosen = call(
        select_kernel,
        geo,
        tuple(shape((per_mate * local, padded), BF16) for _ in range(width)),
        (counts, fresh, *column),
        hbm=1,
        after=1,
        us=20,
        scratch=[
            pltpu.VMEM((hops * prompts, local, padded), BF16),
            pltpu.SMEM(counts.shape, jnp.int32),
            pltpu.SemaphoreType.DMA(()),
        ],
    )
    products = call(
        state_kernel,
        geo,
        shape(fan, BF16),
        (kda_prefill, counts, *chosen, got),
        hbm=2,
        after=width,
        us=20,
        scratch=[
            pltpu.VMEM(kda_prefill.shape, BF16),
            pltpu.VMEM(fan, BF16),
            pltpu.VMEM(fan, BF16),
            pltpu.SMEM(counts.shape, jnp.int32),
            pltpu.SemaphoreType.DMA((parts + 1,)),
        ],
    )
    back = lax.all_to_all(products, "roll", 0, 0, tiled=True)
    taken = [lax.ppermute(chosen[s], "roll", mates(-1, s)) for s in range(1, width)]
    taken = [chosen[0], *hold(taken, products)]
    caches = []
    for piece in taken:
        caches.append(piece)
        for e in range(1, halves):
            caches.append(
                lax.ppermute(piece, "exp", [(i, (i - e) % halves) for i in range(halves)])
            )
    cols = pad_to(per_mate * (cache + steps), 128)
    mla_out = call(
        latent_kernel,
        geo,
        shape((rows, heads * dv), BF16),
        (w_uv, counts, prompt_len, products, queries, fresh, *caches),
        hbm=3,
        after=1,
        us=0,
        mib=32,
        scratch=[
            pltpu.VMEM((cols, padded), BF16),
            pltpu.VMEM((heads, rows, rank), BF16),
            pltpu.VMEM((rows, heads * dv), BF16),
            pltpu.VMEM(w_uv.shape, BF16),
            pltpu.SMEM(counts.shape, jnp.int32),
            pltpu.SMEM(prompt_len.shape, jnp.int32),
            pltpu.SemaphoreType.DMA((3,)),
        ],
    )
    kda_out = call(
        kda_out_kernel, geo, shape((steps, per, kda_width), BF16), (kda_v, mla_out, back, coef), hbm=1, after=1,
        scratch=[pltpu.VMEM(kda_v.shape, BF16), pltpu.SemaphoreType.DMA(())],
    )
    return (kda_out, mla_out.reshape(steps, per, heads * dv))


def solution(mesh):
    return jax.shard_map(
        on_device,
        mesh=mesh,
        in_specs=(
            P("roll", "exp", None, None),
            P("roll", "exp", None),
            P(),
            P(),
            P(None, "roll", "exp"),
            P(None, "roll", "exp"),
            P(None, "roll", "exp"),
            P(None, "roll", "exp"),
            P(None, "roll", "exp"),
            P(None, "roll", "exp"),
            P(None, "roll", None),
            P("exp", None, None),
        ),
        out_specs=(P(None, "roll", "exp"), P(None, "roll", "exp")),
        check_vma=False,
    )
```

```python
import functools

import jax
import jax.numpy as jnp
from jax import lax
from jax.experimental import pallas as pl
from jax.experimental.pallas import tpu as pltpu
from jax.sharding import PartitionSpec as P

F32 = jnp.float32
BF16 = jnp.bfloat16
NEG = -1e30


def split(x, n):
    if n & (n - 1) == 0:
        return lax.shift_right_logical(x, jnp.full_like(x, n.bit_length() - 1)), x & (n - 1)
    return lax.div(x, jnp.full_like(x, n)), lax.rem(x, jnp.full_like(x, n))


def wrap(x, n):
    return jnp.where(x < 0, x + n, x)


def lanes(shape, dim):
    return lax.broadcasted_iota(jnp.int32, shape, dim)


def prompt_at(counts_ref, owner, j):
    bound = jnp.int32(0)
    k = jnp.zeros_like(j)
    for i in range(counts_ref.shape[0]):
        bound = bound + counts_ref[i, owner]
        k = k + (bound <= j).astype(jnp.int32)
    return k


def fan_rows(geo, shape, dim, me):
    group, slots, steps, parts, per = (geo[n] for n in ("group", "slots", "steps", "parts", "per"))
    other, rest = split(lanes(shape, dim), parts * slots * steps)
    part, rest = split(rest, slots * steps)
    slot, step = split(rest, steps)
    j = wrap(other - me, group) + group * slot
    return part, jnp.where(j < per, step * per + j, -1)


def one_hot(hit):
    return hit.astype(F32).astype(BF16)


def dot(a, b):
    return lax.dot_general(a, b, (((1,), (0,)), ((), ())), preferred_element_type=F32)


def dot_first(a, b):
    return lax.dot_general(a, b, (((0,), (0,)), ((), ())), preferred_element_type=F32)


def dot_t(a, b):
    return lax.dot_general(a, b, (((1,), (1,)), ((), ())), preferred_element_type=F32)


def row_sums(x, ones):
    return dot(x.astype(BF16), ones)


def slot_sample(geo, hop, pair, carry):
    return wrap(hop - carry, geo["depth"]) + geo["depth"] * pair


def fill_table(geo, counts_ref, table_ref):
    width, depth, prompts, pairs = (geo[n] for n in ("width", "depth", "prompts", "pairs"))
    a, b = split(lax.axis_index("roll"), width)
    at = 0
    for s in range(width):
        for hop in geo["order"]:
            if hop == 0:
                column = wrap(b + s - width, width)
                carry = (b + s >= width).astype(jnp.int32)
                owner, piece = a * width + column, s
            else:
                carry = (b < s).astype(jnp.int32)
                owner = wrap(a + hop - depth, depth) * width + b
                piece = hop - 1
            for pair in range(pairs):
                j = s + width * slot_sample(geo, hop, pair, carry)
                k = jnp.minimum(prompt_at(counts_ref, owner, j), prompts - 1)
                table_ref[at] = piece * prompts + k
                at += 1


def reads_kernel(geo, q_hbm, k_hbm, g_hbm, v_hbm, b_hbm, c_hbm, r_ref, a_ref, table_ref, *scratch):
    q_ref, k_ref, g_ref, v_ref, b_ref, raw, counts_ref, sems = scratch
    _, per, width = q_ref.shape
    heads = geo["heads"]
    dk = width // heads
    parts = geo["parts"]
    wide = width // parts
    unit = 2 * dk
    chunk = width // 2
    beta_copy = pltpu.make_async_copy(b_hbm, b_ref, sems.at[2, 0])
    beta_copy.start()
    counts_copy = pltpu.make_async_copy(c_hbm, counts_ref, sems.at[2, 1])
    counts_copy.start()
    copies = []
    for c in range(2):
        sl = pl.ds(c * chunk, chunk)
        pairs = ((q_hbm, q_ref), (k_hbm, k_ref), (g_hbm, g_ref), (v_hbm, v_ref))
        for n, (src, dst) in enumerate(pairs):
            copies.append(pltpu.make_async_copy(src.at[:, :, sl], dst.at[:, :, sl], sems.at[c, n]))
            copies[-1].start()
    me = lax.axis_index("roll")
    ones = one_hot(split(lanes((unit, unit), 0), dk)[0] == split(lanes((unit, unit), 1), dk)[0])
    rows, rows_in = r_ref.shape[0], raw.shape[0]
    part, place = fan_rows(geo, (rows, rows_in), 0, me)
    pick = one_hot((lanes((rows, rows_in), 1) == part * (2 * per) + place) & (place >= 0))
    spread = one_hot(lanes((heads, width), 0) == split(lanes((heads, width), 1), dk)[0])
    betas = []
    beta_copy.wait()
    for t in range(2):
        beta = b_ref[t]
        high = beta.astype(BF16)
        low = (beta - high.astype(F32)).astype(BF16)
        betas.append(dot_first(high, spread) + dot_first(low, spread))
    for c in range(parts):
        for at in range(c * wide, (c + 1) * wide, unit):
            if at % chunk == 0:
                for copy in copies[4 * (at // chunk) : 4 * (at // chunk) + 4]:
                    copy.wait()
            sl = slice(at, at + unit)
            q1, q2 = q_ref[0, :, sl].astype(F32), q_ref[1, :, sl].astype(F32)
            k1, k2 = k_ref[0, :, sl].astype(F32), k_ref[1, :, sl].astype(F32)
            d1, d2 = jnp.exp(-g_ref[0, :, sl]), jnp.exp(-g_ref[1, :, sl])
            dq2, dk2 = d2 * q2, d2 * k2
            terms = (q1 * q1, k1 * k1, q2 * q2, k2 * k2, k1 * q1, k2 * q2, k1 * dq2, k1 * dk2)
            sums = row_sums(jnp.concatenate(terms, axis=0), ones)
            s = [sums[n * per : (n + 1) * per] for n in range(8)]
            rq1, rk1, rq2, rk2 = (lax.rsqrt(x + 1e-06) for x in s[:4])
            b1, b2 = betas[0][:, sl], betas[1][:, sl]
            a11 = b1 * (s[4] * rk1 * rq1)
            a22 = b2 * (s[5] * rk2 * rq2)
            a22k = a22 * rk2
            a21 = b1 * (rk1 * (rq2 * s[6] - a22k * s[7]))
            r1 = d1 * (rq1 * q1 - (a11 * rk1) * k1)
            r2 = d1 * (rq2 * dq2 - a22k * dk2 - (a21 * rk1) * k1)
            to = slice(at - c * wide, at - c * wide + unit)
            raw[2 * c * per : (2 * c + 1) * per, to] = r1.astype(BF16)
            raw[(2 * c + 1) * per : (2 * c + 2) * per, to] = r2.astype(BF16)
            v1, v2 = v_ref[0, :, sl].astype(F32), v_ref[1, :, sl].astype(F32)
            a_ref[0, :, sl] = a11 * v1
            a_ref[1, :, sl] = a21 * v1 + a22 * v2
    r_ref[...] = dot(pick, raw[...]).astype(BF16)
    counts_copy.wait()
    fill_table(geo, counts_ref, table_ref)


def state_kernel(geo, s_hbm, c_hbm, *refs):
    r_hbm, y_ref, r_ref, s_ref, r_all, y_all, counts_ref, sems = refs[-8:]
    rows, wide = r_ref.shape
    prompts, heads, dk, dv = s_ref.shape
    me = lax.axis_index("roll")
    group, slots, steps, parts = geo["group"], geo["slots"], geo["steps"], geo["parts"]
    first = pltpu.make_async_copy(r_hbm, r_ref, sems.at[parts + 1])
    first.start()
    copies = [pltpu.make_async_copy(c_hbm, counts_ref, sems.at[parts])]
    for c in range(parts):
        sl = pl.ds(c * (heads // parts), heads // parts)
        copies.append(pltpu.make_async_copy(s_hbm.at[:, sl], s_ref.at[:, sl], sems.at[c]))
    for copy in copies:
        copy.start()
    few, own = rows // parts, slots * steps
    part, rest = split(lanes((rows, rows), 0), few)
    other, rest = split(rest, own)
    sort = one_hot(lanes((rows, rows), 1) == (other * parts + part) * own + rest)
    part, rest = split(lanes((rows, rows), 1), few)
    other, rest = split(rest, own)
    back = one_hot(lanes((rows, rows), 0) == (other * parts + part) * own + rest)
    first.wait()
    r_all[...] = dot(sort, r_ref[...]).astype(BF16)
    copies[0].wait()
    other, rest = split(lanes((few, dk), 0), own)
    j = wrap(me - other, group) + group * split(rest, steps)[0]
    k = prompt_at(counts_ref, me, j)
    keep = [one_hot(k == p) for p in range(prompts)]
    for c in range(parts):
        copies[1 + c].wait()
        for at in range(wide // dk):
            h = c * (wide // dk) + at
            r = r_all[c * few : (c + 1) * few, at * dk : (at + 1) * dk]
            acc = dot(r * keep[0], s_ref[0, h])
            for p in range(1, prompts):
                acc = acc + dot(r * keep[p], s_ref[p, h])
            y_all[c * few : (c + 1) * few, at * dv : (at + 1) * dv] = acc.astype(BF16)
    y_ref[...] = dot(back, y_all[...]).astype(BF16)


def kda_out_kernel(geo, y_hbm, _, a_ref, o_hbm, y_ref, o_ref, sems):
    per, parts = geo["per"], geo["parts"]
    rows, wide = y_ref.shape
    copy = pltpu.make_async_copy(y_hbm, y_ref, sems.at[0])
    copy.start()
    me = lax.axis_index("roll")
    shape = (2 * per * parts, rows)
    part, place = fan_rows(geo, shape, 1, me)
    pick = one_hot((lanes(shape, 0) == part * (2 * per) + place) & (place >= 0))
    copy.wait()
    send = []
    for c in range(parts):
        sl = pl.ds(c * wide, wide)
        y = dot(pick[2 * c * per : 2 * (c + 1) * per], y_ref[...])
        for t in range(2):
            o_ref[t, :, sl] = (y[t * per : (t + 1) * per] + a_ref[t, :, sl]).astype(BF16)
        send.append(pltpu.make_async_copy(o_ref.at[:, :, sl], o_hbm.at[:, :, sl], sems.at[1 + c]))
        send[c].start()
    for copy in send:
        copy.wait()


def select_kernel(geo, table_ref, *refs):
    width, order, prompts, pairs, entry = (
        geo[n] for n in ("width", "order", "prompts", "pairs", "entry")
    )
    o_refs, plane_pool, column_pool = refs[-2 - width : -2], *refs[-2:]
    column, plane = refs[: -2 - 2 * width], refs[-2 - 2 * width : -2 - width]
    for pool, pieces in ((plane_pool, plane), (column_pool, column)):
        pool[:, :, entry:] = jnp.zeros(pool.shape[:2] + (pool.shape[2] - entry,), BF16)
        for n, piece in enumerate(pieces):
            pool[n * prompts : (n + 1) * prompts, :, :entry] = piece[...]
    local = plane_pool.shape[1]
    sent = len(column) * pairs * local
    at = 0
    for s in range(width):
        to = 0
        for hop in order:
            for pair in range(pairs):
                if hop == 0:
                    o_ref, rows, pool = o_refs[0], sent + (s * pairs + pair) * local, plane_pool
                else:
                    o_ref, rows, pool = o_refs[s], to * local, column_pool
                    to += 1
                o_ref[rows : rows + local, :] = pool[table_ref[at]]
                at += 1


def query_kernel(geo, q_hbm, f_hbm, c_hbm, l_hbm, _, o_ref, n_ref, length_ref, *scratch):
    q_ref, f_ref, counts_ref, len_ref, sems = scratch
    total, wide = q_ref.shape
    width, per, steps, entry = geo["width"], geo["per"], geo["steps"], geo["entry"]
    group, prompts, per_mate = (geo[n] for n in ("group", "prompts", "per_mate"))
    padded = o_ref.shape[1]
    heads = wide // entry
    unit = 2 * entry
    n = total // width
    small = [
        pltpu.make_async_copy(src, dst, sems.at[heads // 2 + x])
        for x, (src, dst) in enumerate(((f_hbm, f_ref), (c_hbm, counts_ref), (l_hbm, len_ref)))
    ]
    copies = []
    for c in range(heads // 2):
        sl = pl.ds(c * unit, unit)
        copies.append(pltpu.make_async_copy(q_hbm.at[:, sl], q_ref.at[:, sl], sems.at[c]))
    for copy in small + copies:
        copy.start()
    row, col = lanes((total, total), 0), lanes((total, total), 1)
    shift, rest = split(row, n)
    i, step = split(rest, steps)
    pick = one_hot(col == step * per + shift + width * i)
    block = n_ref.shape[0] // width
    n_ref[...] = jnp.zeros(n_ref.shape, BF16)
    me = lax.axis_index("roll")
    sample = split(lanes((n, length_ref.shape[1]), 0), steps)[0]
    for copy in small:
        copy.wait()
    for s in range(width):
        length = jnp.zeros(sample.shape, jnp.int32)
        for i in range(per_mate):
            j = jnp.int32(s + width * i)
            owner = split(me + j, group)[1]
            k = prompt_at(counts_ref, owner, j)
            length = jnp.where(sample == i, len_ref[owner * prompts + k], length)
        length_ref[s * n : (s + 1) * n, :] = length
    out = dot(pick, f_ref[...]).astype(BF16)
    for s in range(width):
        n_ref[s * block : s * block + n, :entry] = out[s * n : (s + 1) * n]
    for c, copy in enumerate(copies):
        copy.wait()
        out = dot(pick, q_ref[:, c * unit : (c + 1) * unit])
        even = out[:, :padded].astype(BF16)
        odd = pltpu.roll(out[:, unit - padded :], entry, 1).astype(BF16)
        for s in range(width):
            at = (s * heads + 2 * c) * n
            o_ref[at : at + n, :] = even[s * n : (s + 1) * n]
            o_ref[at + n : at + 2 * n, :] = odd[s * n : (s + 1) * n]


def latent_kernel(geo, w_hbm, *refs):
    width, steps, per, per_mate = (geo[n] for n in ("width", "steps", "per", "per_mate"))
    halves, local, pairs, order = (geo[n] for n in ("halves", "local", "pairs", "order"))
    arrays = halves * width
    k_hbm, refs = refs[:arrays], refs[arrays:]
    _, q_ref, n_ref, length_ref, o_hbm, keys, ctx, out, w_ref, o_ref, sems = refs
    heads, rank, dv = w_ref.shape
    half = lax.axis_index("exp")
    few = pairs * local
    sent = (len(order) - 1) * few
    piece = sent + few
    old = halves * piece
    n = per_mate * steps
    block = n_ref.shape[0] // width
    copies = []
    for s in range(width):
        for e in range(halves):
            first = k_hbm[e].at[pl.ds(sent + s * few, few)], keys.at[s, pl.ds(e * piece + sent, few)]
            rest = k_hbm[s * halves + e].at[pl.ds(0, sent)], keys.at[s, pl.ds(e * piece, sent)]
            for src, dst in (rest, first):
                copies.append(pltpu.make_async_copy(src, dst, sems.at[len(copies)]))
    each = len(copies) // width
    copies.append(pltpu.make_async_copy(w_hbm, w_ref, sems.at[len(copies)]))
    for copy in copies:
        copy.start()
    _, b = split(lax.axis_index("roll"), width)
    row, col = lanes((n, old), 0), lanes((n, old), 1)
    e, rest = split(col, piece)
    rest, pos = split(rest, local)
    place, pair = split(rest, pairs)
    hop = jnp.zeros_like(place)
    for x, h in enumerate(order):
        hop = jnp.where(place == x, h, hop)
    e = e + half
    pos = jnp.where(e >= halves, e - halves, e) * local + pos
    of_carry = []
    for carry in range(2):
        other = slot_sample(geo, hop, pair, carry)
        mine = (other == split(row, steps)[0]) & (other < per_mate)
        of_carry.append(jnp.where(mine, pos, halves * local))
    row, col = lanes((n, block), 0), lanes((n, block), 1)
    behind = row - col
    allowed_new = ((behind >= 0) & (behind <= split(row, steps)[1]))[None]
    scores = []
    for s in range(width):
        query = q_ref[s * heads * n : (s + 1) * heads * n, :]
        keys[s, old:, :] = n_ref[s * block : (s + 1) * block, :]
        for copy in copies[s * each : (s + 1) * each]:
            copy.wait()
        scores.append(dot_t(query, keys[s]).reshape(heads, n, old + block) * geo["scale"])
    weights = []
    for s in range(width):
        length = length_ref[s * n : (s + 1) * n, :]
        length = jnp.concatenate([length] * -(-old // length.shape[1]), axis=1)[:, :old]
        pos = jnp.where(b + s >= width, of_carry[1], of_carry[0])
        allowed_old = (pos < length)[None]
        part = jnp.concatenate(
            [
                jnp.where(allowed_old, scores[s][:, :, :old], NEG),
                jnp.where(allowed_new, scores[s][:, :, old:], NEG),
            ],
            axis=-1,
        )
        top = jnp.max(part, axis=-1, keepdims=True)
        raised = jnp.exp(part - top)
        part = raised / jnp.sum(raised, axis=-1, keepdims=True)
        weights.append(part.reshape(heads * n, old + block).astype(BF16))
    for s in range(width):
        context = dot(weights[s], keys[s, :, :rank]).astype(BF16)
        for h in range(heads):
            ctx[h, s * n : (s + 1) * n, :] = context[h * n : (h + 1) * n]
    copies[-1].wait()
    for h in range(heads):
        out[:, h * dv : (h + 1) * dv] = dot(ctx[h], w_ref[h]).astype(BF16)
    rows = steps * per
    shift, rest = split(lanes((rows, rows), 1), n)
    sample, step = split(rest, steps)
    place = step * per + shift + width * sample
    pick = one_hot(lanes((rows, rows), 0) == place)
    send = []
    for c in range(2):
        sl = pl.ds(c * (heads * dv // 2), heads * dv // 2)
        o_ref[:, sl] = dot(pick, out[:, sl]).astype(BF16)
        send.append(pltpu.make_async_copy(o_ref.at[:, sl], o_hbm.at[:, sl], sems.at[c]))
        send[c].start()
    for copy in send:
        copy.wait()


def cost(us):
    return pl.CostEstimate(
        flops=2_000_000_000 * us, bytes_accessed=3_000_000 * us, transcendentals=20_000_000 * us
    )


def call(kernel, geo, out, args, smem=0, hbm=0, after=0, scratch=(), mib=16, us=0):
    spaces = [pltpu.SMEM] * smem + [pltpu.HBM] * hbm + [pl.ANY] * after
    spaces += [pltpu.VMEM] * (len(args) - len(spaces))

    def place(x):
        if isinstance(x, jax.ShapeDtypeStruct):
            return pl.BlockSpec(memory_space=pltpu.SMEM if len(x.shape) == 1 else pltpu.VMEM)
        return pl.BlockSpec(memory_space=pltpu.HBM)

    outs = jax.tree.map(place, out)
    args = [
        pltpu.with_memory_space_constraint(x, pltpu.HBM) if s == pltpu.HBM else x
        for x, s in zip(args, spaces, strict=True)
    ]
    return pl.pallas_call(
        functools.partial(kernel, geo),
        out_shape=out,
        in_specs=[pl.BlockSpec(memory_space=s) for s in spaces],
        out_specs=outs,
        scratch_shapes=list(scratch),
        cost_estimate=cost(us),
        compiler_params=pltpu.CompilerParams(vmem_limit_bytes=mib * 1024 * 1024),
        name=kernel.__name__,
    )(*args)


def hold(x, first):
    return pl.pallas_call(
        lambda *refs: None,
        out_shape=tuple(jax.ShapeDtypeStruct(a.shape, a.dtype) for a in x),
        in_specs=[pl.BlockSpec(memory_space=pl.ANY)] * (len(x) + 1),
        out_specs=[pl.BlockSpec(memory_space=pl.ANY)] * len(x),
        input_output_aliases={n + 1: n for n in range(len(x))},
        cost_estimate=cost(20),
        name="hold",
    )(first, *x)


def pad_to(n, m):
    return -(-n // m) * m


def on_device(
    kda_prefill,
    latent_prefill,
    prompt_len,
    sample_counts,
    kda_q,
    kda_k,
    kda_v,
    kda_decay,
    kda_beta,
    mla_q,
    mla_new,
    w_uv,
):
    group = lax.axis_size("roll")
    halves = lax.axis_size("exp")
    steps, per, kda_width = kda_q.shape
    heads = kda_beta.shape[2]
    prompts, local, entry = latent_prefill.shape
    cache = local * halves
    _, rank, dv = w_uv.shape
    width = 4
    depth = group // width
    slots = -(-per // group)
    per_mate = per // width
    hops = min(depth, per_mate + 1)
    padded = pad_to(entry, 128)
    parts = max(1, min(16 // (slots * steps), heads // 2))
    geo = dict(
        group=group,
        halves=halves,
        steps=steps,
        per=per,
        width=width,
        depth=depth,
        slots=slots,
        hops=hops,
        prompts=prompts,
        cache=cache,
        entry=entry,
        per_mate=per_mate,
        local=local,
        pairs=max(-(-per_mate // depth), -(-16 // local)),
        order=[*range(1, hops), 0],
        scale=192.0**-0.5,
        heads=heads,
        parts=parts,
    )
    shape = jax.ShapeDtypeStruct

    def mates(sign, s):
        return [(i, i // width * width + (i + sign * s) % width) for i in range(group)]

    counts = sample_counts.T
    fan = (group * parts * slots * steps, kda_width // parts)
    reads, coef, table = call(
        reads_kernel,
        geo,
        (
            shape(fan, BF16),
            shape((steps, per, kda_width), F32),
            shape((width * hops * geo["pairs"],), jnp.int32),
        ),
        (kda_q, kda_k, kda_decay, kda_v, jnp.swapaxes(kda_beta, 1, 2), counts),
        hbm=6,
        scratch=[
            pltpu.VMEM(kda_q.shape, BF16),
            pltpu.VMEM(kda_q.shape, BF16),
            pltpu.VMEM(kda_q.shape, F32),
            pltpu.VMEM(kda_q.shape, BF16),
            pltpu.VMEM((steps, heads, per), F32),
            pltpu.VMEM((steps * per * parts, kda_width // parts), BF16),
            pltpu.SMEM(counts.shape, jnp.int32),
            pltpu.SemaphoreType.DMA((3, 4)),
        ],
    )
    got = lax.all_to_all(reads, "roll", 0, 0, tiled=True)

    plane = [latent_prefill] + [
        lax.ppermute(latent_prefill, "roll", mates(-1, s)) for s in range(1, width)
    ]
    column = [
        lax.ppermute(latent_prefill, "roll", [(i, (i - width * h) % group) for i in range(group)])
        for h in range(1, hops)
    ]
    few = geo["pairs"] * local
    sent = (hops - 1) * few
    wide = mla_q.shape[2]
    rows = steps * per
    few = geo["pairs"] * local
    sent = (hops - 1) * few
    wide = mla_q.shape[2]
    rows = steps * per
    queries, fresh, lengths = call(
        query_kernel,
        geo,
        (
            shape((heads * rows, padded), BF16),
            shape((width * pad_to(per_mate * steps, 128), padded), BF16),
            shape((rows, 128), jnp.int32),
        ),
        (mla_q.reshape(rows, wide), mla_new.reshape(rows, entry), counts, prompt_len, reads),
        hbm=4,
        after=1,
        scratch=[
            pltpu.VMEM((rows, wide), BF16),
            pltpu.VMEM((rows, entry), BF16),
            pltpu.SMEM(counts.shape, jnp.int32),
            pltpu.SMEM(prompt_len.shape, jnp.int32),
            pltpu.SemaphoreType.DMA((heads // 2 + 3,)),
        ],
    )
    chosen = call(
        select_kernel,
        geo,
        tuple(shape((sent + (s == 0) * width * few, padded), BF16) for s in range(width)),
        (table, *column, *plane),
        smem=1,
        us=20,
        scratch=[
            pltpu.VMEM((width * prompts, local, padded), BF16),
            pltpu.VMEM(((hops - 1) * prompts, local, padded), BF16),
        ],
    )
    products = call(
        state_kernel,
        geo,
        shape(fan, BF16),
        (kda_prefill, counts, *chosen, got),
        hbm=2,
        after=len(chosen) + 1,
        us=20,
        scratch=[
            pltpu.VMEM(fan, BF16),
            pltpu.VMEM(kda_prefill.shape, BF16),
            pltpu.VMEM(fan, BF16),
            pltpu.VMEM(fan, BF16),
            pltpu.SMEM(counts.shape, jnp.int32),
            pltpu.SemaphoreType.DMA((parts + 2,)),
        ],
    )
    back = lax.all_to_all(products, "roll", 0, 0, tiled=True)
    taken = [lax.ppermute(chosen[s], "roll", mates(-1, s)) for s in range(1, width)]
    taken = [chosen[0], *hold(taken, products)]
    caches = []
    for piece in taken:
        caches.append(piece)
        for e in range(1, halves):
            caches.append(
                lax.ppermute(piece, "exp", [(i, (i - e) % halves) for i in range(halves)])
            )
    mla_out = call(
        latent_kernel,
        geo,
        pltpu.HBM((rows, heads * dv), BF16),
        (w_uv, *caches, products, queries, fresh, lengths),
        hbm=1,
        after=1 + len(caches),
        scratch=[
            pltpu.VMEM((width, fresh.shape[0] // width + hops * few * halves, padded), BF16),
            pltpu.VMEM((heads, rows, rank), BF16),
            pltpu.VMEM((rows, heads * dv), BF16),
            pltpu.VMEM(w_uv.shape, BF16),
            pltpu.VMEM((rows, heads * dv), BF16),
            pltpu.SemaphoreType.DMA((width * halves * 2 + 1,)),
        ],
    )
    kda_out = call(
        kda_out_kernel,
        geo,
        pltpu.HBM((steps, per, kda_width), BF16),
        (back, mla_out, coef),
        hbm=2,
        scratch=[
            pltpu.VMEM(fan, BF16),
            pltpu.VMEM((steps, per, kda_width), BF16),
            pltpu.SemaphoreType.DMA((parts + 1,)),
        ],
    )
    return (kda_out, mla_out.reshape(steps, per, heads * dv))


def solution(mesh):
    return jax.shard_map(
        on_device,
        mesh=mesh,
        in_specs=(
            P("roll", "exp", None, None),
            P("roll", "exp", None),
            P(),
            P(),
            P(None, "roll", "exp"),
            P(None, "roll", "exp"),
            P(None, "roll", "exp"),
            P(None, "roll", "exp"),
            P(None, "roll", "exp"),
            P(None, "roll", "exp"),
            P(None, "roll", None),
            P("exp", None, None),
        ),
        out_specs=(P(None, "roll", "exp"), P(None, "roll", "exp")),
        check_vma=False,
    )
```

```python
import functools

import jax
import jax.numpy as jnp
from jax import lax
from jax.experimental import pallas as pl
from jax.experimental.pallas import tpu as pltpu
from jax.sharding import PartitionSpec as P

F32 = jnp.float32
BF16 = jnp.bfloat16
NEG = -1e30


def split(x, n):
    if n & (n - 1) == 0:
        return lax.shift_right_logical(x, jnp.full_like(x, n.bit_length() - 1)), x & (n - 1)
    return lax.div(x, jnp.full_like(x, n)), lax.rem(x, jnp.full_like(x, n))


def wrap(x, n):
    return jnp.where(x < 0, x + n, x)


def lanes(shape, dim):
    return lax.broadcasted_iota(jnp.int32, shape, dim)


def prompt_at(counts_ref, owner, j):
    bound = jnp.int32(0)
    k = jnp.zeros_like(j)
    for i in range(counts_ref.shape[0]):
        bound = bound + counts_ref[i, owner]
        k = k + (bound <= j).astype(jnp.int32)
    return k


def fan_rows(geo, shape, dim, me):
    group, slots, steps, parts, per = (geo[n] for n in ("group", "slots", "steps", "parts", "per"))
    other, rest = split(lanes(shape, dim), parts * slots * steps)
    part, rest = split(rest, slots * steps)
    slot, step = split(rest, steps)
    j = wrap(other - me, group) + group * slot
    return part, jnp.where(j < per, step * per + j, -1)


def one_hot(hit):
    return hit.astype(F32).astype(BF16)


def dot(a, b):
    return lax.dot_general(a, b, (((1,), (0,)), ((), ())), preferred_element_type=F32)


def dot_first(a, b):
    return lax.dot_general(a, b, (((0,), (0,)), ((), ())), preferred_element_type=F32)


def dot_t(a, b):
    return lax.dot_general(a, b, (((1,), (1,)), ((), ())), preferred_element_type=F32)


def row_sums(x, ones):
    return dot(x.astype(BF16), ones)


def slot_sample(geo, hop, pair, carry):
    return wrap(hop - carry, geo["depth"]) + geo["depth"] * pair


def fill_table(geo, counts_ref, table_ref):
    width, depth, prompts, pairs = (geo[n] for n in ("width", "depth", "prompts", "pairs"))
    a, b = split(lax.axis_index("roll"), width)
    at = 0
    for s in range(width):
        for hop in geo["order"]:
            if hop == 0:
                column = wrap(b + s - width, width)
                carry = (b + s >= width).astype(jnp.int32)
                owner, piece = a * width + column, s
            else:
                carry = (b < s).astype(jnp.int32)
                owner = wrap(a + hop - depth, depth) * width + b
                piece = hop - 1
            for pair in range(pairs):
                j = s + width * slot_sample(geo, hop, pair, carry)
                k = jnp.minimum(prompt_at(counts_ref, owner, j), prompts - 1)
                table_ref[at] = piece * prompts + k
                at += 1


def reads_kernel(geo, q_hbm, k_hbm, g_hbm, v_hbm, b_hbm, c_hbm, r_ref, a_ref, table_ref, *scratch):
    q_ref, k_ref, g_ref, v_ref, b_ref, raw, counts_ref, sems = scratch
    _, per, width = q_ref.shape
    heads = geo["heads"]
    dk = width // heads
    parts = geo["parts"]
    wide = width // parts
    unit = 2 * dk
    chunk = width // 2
    beta_copy = pltpu.make_async_copy(b_hbm, b_ref, sems.at[2, 0])
    beta_copy.start()
    counts_copy = pltpu.make_async_copy(c_hbm, counts_ref, sems.at[2, 1])
    counts_copy.start()
    copies = []
    for c in range(2):
        sl = pl.ds(c * chunk, chunk)
        pairs = ((q_hbm, q_ref), (k_hbm, k_ref), (g_hbm, g_ref), (v_hbm, v_ref))
        for n, (src, dst) in enumerate(pairs):
            copies.append(pltpu.make_async_copy(src.at[:, :, sl], dst.at[:, :, sl], sems.at[c, n]))
            copies[-1].start()
    me = lax.axis_index("roll")
    ones = one_hot(split(lanes((unit, unit), 0), dk)[0] == split(lanes((unit, unit), 1), dk)[0])
    rows, rows_in = r_ref.shape[0], raw.shape[0]
    part, place = fan_rows(geo, (rows, rows_in), 0, me)
    pick = one_hot((lanes((rows, rows_in), 1) == part * (2 * per) + place) & (place >= 0))
    spread = one_hot(lanes((heads, width), 0) == split(lanes((heads, width), 1), dk)[0])
    betas = []
    beta_copy.wait()
    for t in range(2):
        beta = b_ref[t]
        high = beta.astype(BF16)
        low = (beta - high.astype(F32)).astype(BF16)
        betas.append(dot_first(high, spread) + dot_first(low, spread))
    for c in range(parts):
        for at in range(c * wide, (c + 1) * wide, unit):
            if at % chunk == 0:
                for copy in copies[4 * (at // chunk) : 4 * (at // chunk) + 4]:
                    copy.wait()
            sl = slice(at, at + unit)
            q1, q2 = q_ref[0, :, sl].astype(F32), q_ref[1, :, sl].astype(F32)
            k1, k2 = k_ref[0, :, sl].astype(F32), k_ref[1, :, sl].astype(F32)
            d1, d2 = jnp.exp(-g_ref[0, :, sl]), jnp.exp(-g_ref[1, :, sl])
            dq2, dk2 = d2 * q2, d2 * k2
            terms = (q1 * q1, k1 * k1, q2 * q2, k2 * k2, k1 * q1, k2 * q2, k1 * dq2, k1 * dk2)
            sums = row_sums(jnp.concatenate(terms, axis=0), ones)
            s = [sums[n * per : (n + 1) * per] for n in range(8)]
            rq1, rk1, rq2, rk2 = (lax.rsqrt(x + 1e-06) for x in s[:4])
            b1, b2 = betas[0][:, sl], betas[1][:, sl]
            a11 = b1 * (s[4] * rk1 * rq1)
            a22 = b2 * (s[5] * rk2 * rq2)
            a22k = a22 * rk2
            a21 = b1 * (rk1 * (rq2 * s[6] - a22k * s[7]))
            r1 = d1 * (rq1 * q1 - (a11 * rk1) * k1)
            r2 = d1 * (rq2 * dq2 - a22k * dk2 - (a21 * rk1) * k1)
            to = slice(at - c * wide, at - c * wide + unit)
            raw[2 * c * per : (2 * c + 1) * per, to] = r1.astype(BF16)
            raw[(2 * c + 1) * per : (2 * c + 2) * per, to] = r2.astype(BF16)
            v1, v2 = v_ref[0, :, sl].astype(F32), v_ref[1, :, sl].astype(F32)
            a_ref[0, :, sl] = a11 * v1
            a_ref[1, :, sl] = a21 * v1 + a22 * v2
    r_ref[...] = dot(pick, raw[...]).astype(BF16)
    counts_copy.wait()
    fill_table(geo, counts_ref, table_ref)


def fill_pool(pool, pieces, prompts):
    local, entry = pieces[0].shape[1:]
    pool[:, :, entry:] = jnp.zeros(pool.shape[:2] + (pool.shape[2] - entry,), BF16)
    for n, piece in enumerate(pieces):
        pool[n * prompts : (n + 1) * prompts, :, :entry] = piece[...]


def state_kernel(geo, table_ref, s_hbm, c_hbm, own_hbm, *refs):
    pieces, refs = refs[: geo["width"] - 1], refs[-14:]
    r_hbm, y_hbm, o_hbm, y_ref, o_ref, r_ref, s_ref, r_all, y_all, pool = refs[:10]
    parts_ref, counts_ref, sems, piece_sems = refs[10:]
    pieces = [
        pltpu.make_async_copy(piece, parts_ref.at[n], piece_sems.at[n])
        for n, piece in enumerate((own_hbm, *pieces))
    ]
    rows, wide = r_ref.shape
    prompts, heads, dk, dv = s_ref.shape
    me = lax.axis_index("roll")
    group, slots, steps, parts = geo["group"], geo["slots"], geo["steps"], geo["parts"]
    first = pltpu.make_async_copy(r_hbm, r_ref, sems.at[parts + 1])
    first.start()
    copies = [pltpu.make_async_copy(c_hbm, counts_ref, sems.at[parts])]
    for c in range(parts):
        sl = pl.ds(c * (heads // parts), heads // parts)
        copies.append(pltpu.make_async_copy(s_hbm.at[:, sl], s_ref.at[:, sl], sems.at[c]))
    for copy in copies + pieces:
        copy.start()
    few, own = rows // parts, slots * steps
    part, rest = split(lanes((rows, rows), 0), few)
    other, rest = split(rest, own)
    sort = one_hot(lanes((rows, rows), 1) == (other * parts + part) * own + rest)
    part, rest = split(lanes((rows, rows), 1), few)
    other, rest = split(rest, own)
    back = one_hot(lanes((rows, rows), 0) == (other * parts + part) * own + rest)
    first.wait()
    r_all[...] = dot(sort, r_ref[...]).astype(BF16)
    copies[0].wait()
    other, rest = split(lanes((few, dk), 0), own)
    j = wrap(me - other, group) + group * split(rest, steps)[0]
    k = prompt_at(counts_ref, me, j)
    keep = [one_hot(k == p) for p in range(prompts)]
    for c in range(parts):
        copies[1 + c].wait()
        for at in range(wide // dk):
            h = c * (wide // dk) + at
            r = r_all[c * few : (c + 1) * few, at * dk : (at + 1) * dk]
            wide_r = jnp.concatenate([r * k for k in keep], axis=1)
            acc = dot(wide_r, s_ref[:, h].reshape(prompts * dk, dv))
            y_all[c * few : (c + 1) * few, at * dv : (at + 1) * dv] = acc.astype(BF16)
    y_ref[...] = dot(back, y_all[...]).astype(BF16)
    send = [pltpu.make_async_copy(y_ref, y_hbm, sems.at[0])]
    send[0].start()
    for copy in pieces:
        copy.wait()
    width, hops, pairs = geo["width"], geo["hops"], geo["pairs"]
    fill_pool(pool, [parts_ref.at[n] for n in range(width)], prompts)
    local = pool.shape[1]
    for s in range(width):
        for pair in range(pairs):
            at = (s * hops + hops - 1) * pairs + pair
            to = (s * pairs + pair) * local
            o_ref[to : to + local, :] = pool[table_ref[at]]
    send.append(pltpu.make_async_copy(o_ref, o_hbm, piece_sems.at[1]))
    send[1].start()
    for copy in send:
        copy.wait()


def kda_out_kernel(geo, _, y_ref, a_ref, o_hbm, o_ref, sems):
    per, parts = geo["per"], geo["parts"]
    rows, wide = y_ref.shape
    me = lax.axis_index("roll")
    shape = (2 * per * parts, rows)
    part, place = fan_rows(geo, shape, 1, me)
    pick = one_hot((lanes(shape, 0) == part * (2 * per) + place) & (place >= 0))
    send = []
    for c in range(parts):
        sl = pl.ds(c * wide, wide)
        y = dot(pick[2 * c * per : 2 * (c + 1) * per], y_ref[...])
        for t in range(2):
            o_ref[t, :, sl] = (y[t * per : (t + 1) * per] + a_ref[t, :, sl]).astype(BF16)
        send.append(pltpu.make_async_copy(o_ref.at[:, :, sl], o_hbm.at[:, :, sl], sems.at[1 + c]))
        send[c].start()
    for copy in send:
        copy.wait()


def select_kernel(geo, table_ref, _, *refs):
    width, hops, prompts, pairs = (geo[n] for n in ("width", "hops", "prompts", "pairs"))
    pieces, o_refs, pool = refs[: hops - 1], refs[hops - 1 : -1], refs[-1]
    fill_pool(pool, [pieces[geo["column"].index(h)] for h in range(1, hops)], prompts)
    local = pool.shape[1]
    for s, o_ref in enumerate(o_refs):
        for to in range((hops - 1) * pairs):
            at = s * hops * pairs + to
            o_ref[to * local : (to + 1) * local, :] = pool[table_ref[at]]


def query_kernel(geo, q_hbm, f_hbm, c_hbm, l_hbm, _, o_ref, n_ref, length_ref, *scratch):
    q_ref, tall, f_ref, counts_ref, len_ref, sems = scratch
    total, wide = q_ref.shape
    width, per, steps, entry = geo["width"], geo["per"], geo["steps"], geo["entry"]
    group, prompts, per_mate = (geo[n] for n in ("group", "prompts", "per_mate"))
    padded = o_ref.shape[1]
    heads = wide // entry
    unit = 2 * entry
    n = total // width
    small = [
        pltpu.make_async_copy(src, dst, sems.at[heads // 2 + x])
        for x, (src, dst) in enumerate(((f_hbm, f_ref), (c_hbm, counts_ref), (l_hbm, len_ref)))
    ]
    copies = []
    for c in range(heads // 2):
        sl = pl.ds(c * unit, unit)
        copies.append(pltpu.make_async_copy(q_hbm.at[:, sl], q_ref.at[:, sl], sems.at[c]))
    for copy in small + copies:
        copy.start()
    row, col = lanes((total, total), 0), lanes((total, total), 1)
    shift, rest = split(row, n)
    step, i = split(rest, per_mate)
    pick = one_hot(col == step * per + shift + width * i)
    n_ref[:, entry:] = jnp.zeros((total, padded - entry), BF16)
    me = lax.axis_index("roll")
    sample = split(lanes((n, length_ref.shape[1]), 0), per_mate)[1]
    for copy in small:
        copy.wait()
    for s in range(width):
        length = jnp.zeros(sample.shape, jnp.int32)
        for i in range(per_mate):
            j = jnp.int32(s + width * i)
            owner = split(me + j, group)[1]
            k = prompt_at(counts_ref, owner, j)
            length = jnp.where(sample == i, len_ref[owner * prompts + k], length)
        length_ref[s * n : (s + 1) * n, :] = length
    n_ref[:, :entry] = dot(pick, f_ref[...]).astype(BF16)
    for c, copy in enumerate(copies):
        copy.wait()
        tiles = range(c * unit // 128, (c + 1) * unit // 128)
        for k in tiles:
            tall[k] = q_ref[:, k * 128 : (k + 1) * 128].astype(F32)
        for s in range(width):
            out = [
                jnp.concatenate(
                    [tall[k, pl.ds(t * per + s, per_mate, width), :] for t in range(steps)], axis=0
                )
                for k in tiles
            ]
            at = (s * heads + 2 * c) * n
            even = jnp.concatenate(out[: padded // 128], axis=1)
            odd = pltpu.roll(jnp.concatenate(out[-padded // 128 :], axis=1), entry, 1)
            o_ref[at : at + n, :] = even.astype(BF16)
            o_ref[at + n : at + 2 * n, :] = odd.astype(BF16)


def latent_kernel(geo, w_hbm, *refs):
    width, steps, per, per_mate = (geo[n] for n in ("width", "steps", "per", "per_mate"))
    halves, local, pairs, order = (geo[n] for n in ("halves", "local", "pairs", "order"))
    arrays = halves * (width + 1)
    k_hbm, refs = refs[:arrays], refs[arrays:]
    _, q_ref, n_ref, length_ref, o_hbm, keys, ctx, out, w_ref, o_ref, sems = refs
    heads, rank, dv = w_ref.shape
    half = lax.axis_index("exp")
    few = pairs * local
    sent = (len(order) - 1) * few
    piece = sent + few
    old = halves * piece
    n = per_mate * steps
    block = keys.shape[1] - old
    copies = []
    for s in range(width):
        for e in range(halves):
            first = k_hbm[e * (width + 1) + width].at[pl.ds(s * few, few)], keys.at[s, pl.ds(e * piece + sent, few)]
            rest = k_hbm[e * (width + 1) + s], keys.at[s, pl.ds(e * piece, sent)]
            for src, dst in (rest, first):
                copies.append(pltpu.make_async_copy(src, dst, sems.at[len(copies)]))
    each = len(copies) // width
    copies.append(pltpu.make_async_copy(w_hbm, w_ref, sems.at[len(copies)]))
    for copy in copies[:-1]:
        copy.start()
    _, b = split(lax.axis_index("roll"), width)
    row, col = lanes((n, old), 0), lanes((n, old), 1)
    e, rest = split(col, piece)
    rest, pos = split(rest, local)
    place, pair = split(rest, pairs)
    hop = jnp.zeros_like(place)
    for x, h in enumerate(order):
        hop = jnp.where(place == x, h, hop)
    e = e + half
    pos = jnp.where(e >= halves, e - halves, e) * local + pos
    of_carry = []
    for carry in range(2):
        other = slot_sample(geo, hop, pair, carry)
        mine = (other == split(row, per_mate)[1]) & (other < per_mate)
        of_carry.append(jnp.where(mine, pos, halves * local))
    row, col = lanes((n, block), 0), lanes((n, block), 1)
    (step, sample), (step_of, sample_of) = split(row, per_mate), split(col, per_mate)
    allowed_new = ((sample == sample_of) & (step_of <= step))[None]
    scores = []
    for s in range(width):
        query = q_ref[s * heads * n : (s + 1) * heads * n, :]
        keys[s, old : old + n, :] = n_ref[s * n : (s + 1) * n, :]
        keys[s, old + n :, :] = jnp.zeros((block - n, keys.shape[2]), BF16)
        for copy in copies[s * each : (s + 1) * each]:
            copy.wait()
        if s == 0:
            copies[-1].start()
        scores.append(dot_t(query, keys[s]).reshape(heads, n, old + block) * geo["scale"])
    weights = []
    for s in range(width):
        length = length_ref[s * n : (s + 1) * n, :]
        length = jnp.concatenate([length] * -(-old // length.shape[1]), axis=1)[:, :old]
        pos = jnp.where(b + s >= width, of_carry[1], of_carry[0])
        allowed_old = (pos < length)[None]
        part = jnp.concatenate(
            [
                jnp.where(allowed_old, scores[s][:, :, :old], NEG),
                jnp.where(allowed_new, scores[s][:, :, old:], NEG),
            ],
            axis=-1,
        )
        top = jnp.max(part, axis=-1, keepdims=True)
        raised = jnp.exp(part - top)
        part = raised / jnp.sum(raised, axis=-1, keepdims=True)
        weights.append(part.reshape(heads * n, old + block).astype(BF16))
    for s in range(width):
        context = dot(weights[s], keys[s, :, :rank]).astype(BF16)
        for h in range(heads):
            ctx[h, s * n : (s + 1) * n, :] = context[h * n : (h + 1) * n]
    copies[-1].wait()
    for h in range(heads):
        out[:, h * dv : (h + 1) * dv] = dot(ctx[h], w_ref[h]).astype(BF16)
    rows = steps * per
    shift, rest = split(lanes((rows, rows), 1), n)
    step, sample = split(rest, per_mate)
    place = step * per + shift + width * sample
    pick = one_hot(lanes((rows, rows), 0) == place)
    send = []
    for c in range(2):
        sl = pl.ds(c * (heads * dv // 2), heads * dv // 2)
        o_ref[:, sl] = dot(pick, out[:, sl]).astype(BF16)
        send.append(pltpu.make_async_copy(o_ref.at[:, sl], o_hbm.at[:, sl], sems.at[c]))
        send[c].start()
    for copy in send:
        copy.wait()


def cost(us):
    return pl.CostEstimate(
        flops=2_000_000_000 * us, bytes_accessed=3_000_000 * us, transcendentals=20_000_000 * us
    )


def call(kernel, geo, out, args, smem=0, hbm=0, after=0, scratch=(), mib=16, us=0):
    spaces = [pltpu.SMEM] * smem + [pltpu.HBM] * hbm + [pl.ANY] * after
    spaces += [pltpu.VMEM] * (len(args) - len(spaces))

    def place(x):
        if isinstance(x, jax.ShapeDtypeStruct):
            return pl.BlockSpec(memory_space=pltpu.SMEM if len(x.shape) == 1 else pltpu.VMEM)
        return pl.BlockSpec(memory_space=pltpu.HBM)

    outs = jax.tree.map(place, out)
    args = [
        pltpu.with_memory_space_constraint(x, pltpu.HBM) if s == pltpu.HBM else x
        for x, s in zip(args, spaces, strict=True)
    ]
    return pl.pallas_call(
        functools.partial(kernel, geo),
        out_shape=out,
        in_specs=[pl.BlockSpec(memory_space=s) for s in spaces],
        out_specs=outs,
        scratch_shapes=list(scratch),
        cost_estimate=cost(us),
        compiler_params=pltpu.CompilerParams(vmem_limit_bytes=mib * 1024 * 1024),
        name=kernel.__name__,
    )(*args)


def hold(x, first):
    return pl.pallas_call(
        lambda *refs: None,
        out_shape=tuple(jax.ShapeDtypeStruct(a.shape, a.dtype) for a in x),
        in_specs=[pl.BlockSpec(memory_space=pl.ANY)] * (len(x) + 1),
        out_specs=[pl.BlockSpec(memory_space=pl.ANY)] * len(x),
        input_output_aliases={n + 1: n for n in range(len(x))},
        cost_estimate=cost(20),
        name="hold",
    )(first, *x)


def pad_to(n, m):
    return -(-n // m) * m


def on_device(
    kda_prefill,
    latent_prefill,
    prompt_len,
    sample_counts,
    kda_q,
    kda_k,
    kda_v,
    kda_decay,
    kda_beta,
    mla_q,
    mla_new,
    w_uv,
):
    group = lax.axis_size("roll")
    halves = lax.axis_size("exp")
    steps, per, kda_width = kda_q.shape
    heads = kda_beta.shape[2]
    prompts, local, entry = latent_prefill.shape
    cache = local * halves
    _, rank, dv = w_uv.shape
    width = 4
    depth = group // width
    slots = -(-per // group)
    per_mate = per // width
    hops = min(depth, per_mate + 1)
    padded = pad_to(entry, 128)
    parts = max(1, min(16 // (slots * steps), heads // 2))
    geo = dict(
        group=group,
        halves=halves,
        steps=steps,
        per=per,
        width=width,
        depth=depth,
        slots=slots,
        hops=hops,
        prompts=prompts,
        cache=cache,
        entry=entry,
        per_mate=per_mate,
        local=local,
        pairs=max(-(-per_mate // depth), -(-16 // local)),
        order=[*range(1, hops), 0],
        column=[h for h in (3, 1, 2, *range(4, hops)) if h < hops],
        scale=192.0**-0.5,
        heads=heads,
        parts=parts,
    )
    shape = jax.ShapeDtypeStruct

    def mates(sign, s):
        return [(i, i // width * width + (i + sign * s) % width) for i in range(group)]

    counts = sample_counts.T
    fan = (group * parts * slots * steps, kda_width // parts)
    reads, coef, table = call(
        reads_kernel,
        geo,
        (
            shape(fan, BF16),
            shape((steps, per, kda_width), F32),
            shape((width * hops * geo["pairs"],), jnp.int32),
        ),
        (kda_q, kda_k, kda_decay, kda_v, jnp.swapaxes(kda_beta, 1, 2), counts),
        hbm=6,
        scratch=[
            pltpu.VMEM(kda_q.shape, BF16),
            pltpu.VMEM(kda_q.shape, BF16),
            pltpu.VMEM(kda_q.shape, F32),
            pltpu.VMEM(kda_q.shape, BF16),
            pltpu.VMEM((steps, heads, per), F32),
            pltpu.VMEM((steps * per * parts, kda_width // parts), BF16),
            pltpu.SMEM(counts.shape, jnp.int32),
            pltpu.SemaphoreType.DMA((3, 4)),
        ],
    )
    got = lax.all_to_all(reads, "roll", 0, 0, tiled=True)

    plane = [lax.ppermute(latent_prefill, "roll", mates(-1, s)) for s in range(1, width)]
    column = [
        lax.ppermute(latent_prefill, "roll", [(i, (i - width * h) % group) for i in range(group)])
        for h in geo["column"]
    ]
    few = geo["pairs"] * local
    sent = (hops - 1) * few
    wide = mla_q.shape[2]
    rows = steps * per
    few = geo["pairs"] * local
    sent = (hops - 1) * few
    wide = mla_q.shape[2]
    rows = steps * per
    queries, fresh, lengths = call(
        query_kernel,
        geo,
        (
            shape((heads * rows, padded), BF16),
            shape((rows, padded), BF16),
            shape((rows, 128), jnp.int32),
        ),
        (mla_q.reshape(rows, wide), mla_new.reshape(rows, entry), counts, prompt_len, column[0]),
        hbm=4,
        after=1,
        scratch=[
            pltpu.VMEM((rows, wide), BF16),
            pltpu.VMEM((wide // 128, rows, 128), F32),
            pltpu.VMEM((rows, entry), BF16),
            pltpu.SMEM(counts.shape, jnp.int32),
            pltpu.SMEM(prompt_len.shape, jnp.int32),
            pltpu.SemaphoreType.DMA((heads // 2 + 3,)),
        ],
    )
    chosen = call(
        select_kernel,
        geo,
        tuple(shape((sent, padded), BF16) for s in range(width)),
        (table, lengths, *column),
        smem=1,
        after=1,
        us=20,
        scratch=[pltpu.VMEM(((hops - 1) * prompts, local, padded), BF16)],
    )
    products, own = call(
        state_kernel,
        geo,
        (pltpu.HBM(fan, BF16), pltpu.HBM((width * few, padded), BF16)),
        (table, kda_prefill, counts, latent_prefill, *plane, *chosen, got),
        smem=1,
        hbm=3,
        after=len(plane) + len(chosen) + 1,
        us=20,
        scratch=[
            pltpu.VMEM(fan, BF16),
            pltpu.VMEM((width * few, padded), BF16),
            pltpu.VMEM(fan, BF16),
            pltpu.VMEM(kda_prefill.shape, BF16),
            pltpu.VMEM(fan, BF16),
            pltpu.VMEM(fan, BF16),
            pltpu.VMEM((width * prompts, local, padded), BF16),
            pltpu.VMEM((width,) + latent_prefill.shape, BF16),
            pltpu.SMEM(counts.shape, jnp.int32),
            pltpu.SemaphoreType.DMA((parts + 2,)),
            pltpu.SemaphoreType.DMA((width,)),
        ],
    )
    back = lax.all_to_all(products, "roll", 0, 0, tiled=True)
    taken = [lax.ppermute(chosen[s], "roll", mates(-1, s)) for s in range(1, width)]
    taken = [*hold([chosen[0], *taken], products), own]
    caches = list(taken)
    for e in range(1, halves):
        pairs = [(i, (i - e) % halves) for i in range(halves)]
        caches += [lax.ppermute(piece, "exp", pairs) for piece in taken]
    mla_out = call(
        latent_kernel,
        geo,
        pltpu.HBM((rows, heads * dv), BF16),
        (w_uv, *caches, products, queries, fresh, lengths),
        hbm=2 + width,
        after=len(caches) - width,
        scratch=[
            pltpu.VMEM((width, hops * few * halves + pad_to(per_mate * steps, 128), padded), BF16),
            pltpu.VMEM((heads, rows, rank), BF16),
            pltpu.VMEM((rows, heads * dv), BF16),
            pltpu.VMEM(w_uv.shape, BF16),
            pltpu.VMEM((rows, heads * dv), BF16),
            pltpu.SemaphoreType.DMA((width * halves * 2 + 1,)),
        ],
    )
    kda_out = call(
        kda_out_kernel,
        geo,
        pltpu.HBM((steps, per, kda_width), BF16),
        (mla_out, pltpu.with_memory_space_constraint(back, pltpu.VMEM), coef),
        hbm=1,
        scratch=[
            pltpu.VMEM((steps, per, kda_width), BF16),
            pltpu.SemaphoreType.DMA((parts + 1,)),
        ],
    )
    return (kda_out, mla_out.reshape(steps, per, heads * dv))


def solution(mesh):
    return jax.shard_map(
        on_device,
        mesh=mesh,
        in_specs=(
            P("roll", "exp", None, None),
            P("roll", "exp", None),
            P(),
            P(),
            P(None, "roll", "exp"),
            P(None, "roll", "exp"),
            P(None, "roll", "exp"),
            P(None, "roll", "exp"),
            P(None, "roll", "exp"),
            P(None, "roll", "exp"),
            P(None, "roll", None),
            P("exp", None, None),
        ),
        out_specs=(P(None, "roll", "exp"), P(None, "roll", "exp")),
        check_vma=False,
    )
```

```python
import functools

import jax
import jax.numpy as jnp
from jax import lax
from jax.experimental import pallas as pl
from jax.experimental.pallas import tpu as pltpu
from jax.sharding import PartitionSpec as P

F32 = jnp.float32
BF16 = jnp.bfloat16
NEG = -1e30


def split(x, n):
    if n & (n - 1) == 0:
        return lax.shift_right_logical(x, jnp.full_like(x, n.bit_length() - 1)), x & (n - 1)
    return lax.div(x, jnp.full_like(x, n)), lax.rem(x, jnp.full_like(x, n))


def wrap(x, n):
    return jnp.where(x < 0, x + n, x)


def lanes(shape, dim):
    return lax.broadcasted_iota(jnp.int32, shape, dim)


def prompt_at(counts_ref, owner, j):
    bound = jnp.int32(0)
    k = jnp.zeros_like(j)
    for i in range(counts_ref.shape[0]):
        bound = bound + counts_ref[i, owner]
        k = k + (bound <= j).astype(jnp.int32)
    return k


def fan_rows(geo, shape, dim, me):
    group, slots, steps, parts, per = (geo[n] for n in ("group", "slots", "steps", "parts", "per"))
    other, rest = split(lanes(shape, dim), parts * slots * steps)
    part, rest = split(rest, slots * steps)
    slot, step = split(rest, steps)
    j = wrap(other - me, group) + group * slot
    return part, jnp.where(j < per, step * per + j, -1)


def one_hot(hit):
    return hit.astype(F32).astype(BF16)


def dot(a, b):
    return lax.dot_general(a, b, (((1,), (0,)), ((), ())), preferred_element_type=F32)


def dot_first(a, b):
    return lax.dot_general(a, b, (((0,), (0,)), ((), ())), preferred_element_type=F32)


def dot_t(a, b):
    return lax.dot_general(a, b, (((1,), (1,)), ((), ())), preferred_element_type=F32)


def row_sums(x, ones):
    return dot(x.astype(BF16), ones)


def slot_sample(geo, hop, pair, carry):
    return wrap(hop - carry, geo["depth"]) + geo["depth"] * pair


def fill_table(geo, counts_ref, table_ref):
    width, depth, prompts, pairs = (geo[n] for n in ("width", "depth", "prompts", "pairs"))
    a, b = split(lax.axis_index("roll"), width)
    at = 0
    for s in range(width):
        for hop in geo["order"]:
            if hop == 0:
                column = wrap(b + s - width, width)
                carry = (b + s >= width).astype(jnp.int32)
                owner, piece = a * width + column, s
            else:
                carry = (b < s).astype(jnp.int32)
                owner = wrap(a + hop - depth, depth) * width + b
                piece = hop - 1
            for pair in range(pairs):
                j = s + width * slot_sample(geo, hop, pair, carry)
                k = jnp.minimum(prompt_at(counts_ref, owner, j), prompts - 1)
                table_ref[at] = piece * prompts + k
                at += 1


def reads_kernel(geo, q_hbm, k_hbm, g_hbm, v_hbm, b_hbm, c_hbm, r_ref, a_ref, table_ref, *scratch):
    q_ref, k_ref, g_ref, v_ref, b_ref, raw, counts_ref, sems = scratch
    _, per, width = q_ref.shape
    heads = geo["heads"]
    dk = width // heads
    parts = geo["parts"]
    wide = width // parts
    unit = 2 * dk
    chunk = width // 2
    beta_copy = pltpu.make_async_copy(b_hbm, b_ref, sems.at[2, 0])
    beta_copy.start()
    counts_copy = pltpu.make_async_copy(c_hbm, counts_ref, sems.at[2, 1])
    counts_copy.start()
    copies = []
    for c in range(2):
        sl = pl.ds(c * chunk, chunk)
        pairs = ((q_hbm, q_ref), (k_hbm, k_ref), (g_hbm, g_ref), (v_hbm, v_ref))
        for n, (src, dst) in enumerate(pairs):
            copies.append(pltpu.make_async_copy(src.at[:, :, sl], dst.at[:, :, sl], sems.at[c, n]))
            copies[-1].start()
    me = lax.axis_index("roll")
    ones = one_hot(split(lanes((unit, unit), 0), dk)[0] == split(lanes((unit, unit), 1), dk)[0])
    rows, rows_in = r_ref.shape[0], raw.shape[0]
    part, place = fan_rows(geo, (rows, rows_in), 0, me)
    pick = one_hot((lanes((rows, rows_in), 1) == part * (2 * per) + place) & (place >= 0))
    spread = one_hot(lanes((heads, width), 0) == split(lanes((heads, width), 1), dk)[0])
    betas = []
    beta_copy.wait()
    for t in range(2):
        beta = b_ref[t]
        high = beta.astype(BF16)
        low = (beta - high.astype(F32)).astype(BF16)
        betas.append(dot_first(high, spread) + dot_first(low, spread))
    for c in range(parts):
        for at in range(c * wide, (c + 1) * wide, unit):
            if at % chunk == 0:
                for copy in copies[4 * (at // chunk) : 4 * (at // chunk) + 4]:
                    copy.wait()
            sl = slice(at, at + unit)
            q1, q2 = q_ref[0, :, sl].astype(F32), q_ref[1, :, sl].astype(F32)
            k1, k2 = k_ref[0, :, sl].astype(F32), k_ref[1, :, sl].astype(F32)
            d1, d2 = jnp.exp(-g_ref[0, :, sl]), jnp.exp(-g_ref[1, :, sl])
            dq2, dk2 = d2 * q2, d2 * k2
            terms = (q1 * q1, k1 * k1, q2 * q2, k2 * k2, k1 * q1, k2 * q2, k1 * dq2, k1 * dk2)
            sums = row_sums(jnp.concatenate(terms, axis=0), ones)
            s = [sums[n * per : (n + 1) * per] for n in range(8)]
            rq1, rk1, rq2, rk2 = (lax.rsqrt(x + 1e-06) for x in s[:4])
            b1, b2 = betas[0][:, sl], betas[1][:, sl]
            a11 = b1 * (s[4] * rk1 * rq1)
            a22 = b2 * (s[5] * rk2 * rq2)
            a22k = a22 * rk2
            a21 = b1 * (rk1 * (rq2 * s[6] - a22k * s[7]))
            r1 = d1 * (rq1 * q1 - (a11 * rk1) * k1)
            r2 = d1 * (rq2 * dq2 - a22k * dk2 - (a21 * rk1) * k1)
            to = slice(at - c * wide, at - c * wide + unit)
            raw[2 * c * per : (2 * c + 1) * per, to] = r1.astype(BF16)
            raw[(2 * c + 1) * per : (2 * c + 2) * per, to] = r2.astype(BF16)
            v1, v2 = v_ref[0, :, sl].astype(F32), v_ref[1, :, sl].astype(F32)
            a_ref[0, :, sl] = a11 * v1
            a_ref[1, :, sl] = a21 * v1 + a22 * v2
    r_ref[...] = dot(pick, raw[...]).astype(BF16)
    counts_copy.wait()
    fill_table(geo, counts_ref, table_ref)


def fill_pool(pool, pieces, prompts):
    local, entry = pieces[0].shape[1:]
    pool[:, :, entry:] = jnp.zeros(pool.shape[:2] + (pool.shape[2] - entry,), BF16)
    for n, piece in enumerate(pieces):
        pool[n * prompts : (n + 1) * prompts, :, :entry] = piece[...]


def state_kernel(geo, table_ref, s_hbm, c_hbm, own_hbm, *refs):
    pieces, refs = refs[: geo["width"] - 1], refs[-14:]
    r_hbm, y_hbm, o_hbm, y_ref, o_ref, r_ref, s_ref, r_all, y_all, pool = refs[:10]
    parts_ref, counts_ref, sems, piece_sems = refs[10:]
    pieces = [
        pltpu.make_async_copy(piece, parts_ref.at[n], piece_sems.at[n])
        for n, piece in enumerate((own_hbm, *pieces))
    ]
    rows, wide = r_ref.shape
    prompts, heads, dk, dv = s_ref.shape
    me = lax.axis_index("roll")
    group, slots, steps, parts = geo["group"], geo["slots"], geo["steps"], geo["parts"]
    first = pltpu.make_async_copy(r_hbm, r_ref, sems.at[parts + 1])
    first.start()
    copies = [pltpu.make_async_copy(c_hbm, counts_ref, sems.at[parts])]
    for c in range(parts):
        sl = pl.ds(c * (heads // parts), heads // parts)
        copies.append(pltpu.make_async_copy(s_hbm.at[:, sl], s_ref.at[:, sl], sems.at[c]))
    for copy in copies + pieces:
        copy.start()
    few, own = rows // parts, slots * steps
    part, rest = split(lanes((rows, rows), 0), few)
    other, rest = split(rest, own)
    sort = one_hot(lanes((rows, rows), 1) == (other * parts + part) * own + rest)
    part, rest = split(lanes((rows, rows), 1), few)
    other, rest = split(rest, own)
    back = one_hot(lanes((rows, rows), 0) == (other * parts + part) * own + rest)
    first.wait()
    r_all[...] = dot(sort, r_ref[...]).astype(BF16)
    copies[0].wait()
    other, rest = split(lanes((few, dk), 0), own)
    j = wrap(me - other, group) + group * split(rest, steps)[0]
    k = prompt_at(counts_ref, me, j)
    keep = [one_hot(k == p) for p in range(prompts)]
    for c in range(parts):
        copies[1 + c].wait()
        for at in range(wide // dk):
            h = c * (wide // dk) + at
            r = r_all[c * few : (c + 1) * few, at * dk : (at + 1) * dk]
            wide_r = jnp.concatenate([r * k for k in keep], axis=1)
            acc = dot(wide_r, s_ref[:, h].reshape(prompts * dk, dv))
            y_all[c * few : (c + 1) * few, at * dv : (at + 1) * dv] = acc.astype(BF16)
    y_ref[...] = dot(back, y_all[...]).astype(BF16)
    send = [pltpu.make_async_copy(y_ref, y_hbm, sems.at[0])]
    send[0].start()
    for copy in pieces:
        copy.wait()
    width, hops, pairs = geo["width"], geo["hops"], geo["pairs"]
    fill_pool(pool, [parts_ref.at[n] for n in range(width)], prompts)
    local = pool.shape[1]
    for s in range(width):
        for pair in range(pairs):
            at = (s * hops + hops - 1) * pairs + pair
            to = (s * pairs + pair) * local
            o_ref[to : to + local, :] = pool[table_ref[at]]
    send.append(pltpu.make_async_copy(o_ref, o_hbm, piece_sems.at[1]))
    send[1].start()
    for copy in send:
        copy.wait()


def kda_out_kernel(geo, _, y_ref, a_ref, o_hbm, o_ref, sems):
    per, parts = geo["per"], geo["parts"]
    rows, wide = y_ref.shape
    me = lax.axis_index("roll")
    shape = (2 * per * parts, rows)
    part, place = fan_rows(geo, shape, 1, me)
    pick = one_hot((lanes(shape, 0) == part * (2 * per) + place) & (place >= 0))
    send = []
    for c in range(parts):
        sl = pl.ds(c * wide, wide)
        y = dot(pick[2 * c * per : 2 * (c + 1) * per], y_ref[...])
        for t in range(2):
            o_ref[t, :, sl] = (y[t * per : (t + 1) * per] + a_ref[t, :, sl]).astype(BF16)
        send.append(pltpu.make_async_copy(o_ref.at[:, :, sl], o_hbm.at[:, :, sl], sems.at[1 + c]))
        send[c].start()
    for copy in send:
        copy.wait()


def select_kernel(geo, table_ref, _, *refs):
    width, hops, prompts, pairs = (geo[n] for n in ("width", "hops", "prompts", "pairs"))
    pieces, o_refs, pool = refs[: hops - 1], refs[hops - 1 : -1], refs[-1]
    fill_pool(pool, [pieces[geo["column"].index(h)] for h in range(1, hops)], prompts)
    local = pool.shape[1]
    for s, o_ref in enumerate(o_refs):
        for to in range((hops - 1) * pairs):
            at = s * hops * pairs + to
            o_ref[to * local : (to + 1) * local, :] = pool[table_ref[at]]


def query_kernel(geo, q_hbm, f_hbm, c_hbm, l_hbm, _, o_ref, n_ref, length_ref, *scratch):
    q_ref, tall, f_ref, counts_ref, len_ref, sems = scratch
    total, wide = q_ref.shape
    width, per, steps, entry = geo["width"], geo["per"], geo["steps"], geo["entry"]
    group, prompts, per_mate = (geo[n] for n in ("group", "prompts", "per_mate"))
    padded = o_ref.shape[1]
    heads = wide // entry
    unit = 2 * entry
    n = total // width
    small = [
        pltpu.make_async_copy(src, dst, sems.at[heads // 2 + x])
        for x, (src, dst) in enumerate(((f_hbm, f_ref), (c_hbm, counts_ref), (l_hbm, len_ref)))
    ]
    copies = []
    for c in range(heads // 2):
        sl = pl.ds(c * unit, unit)
        copies.append(pltpu.make_async_copy(q_hbm.at[:, sl], q_ref.at[:, sl], sems.at[c]))
    for copy in small + copies:
        copy.start()
    row, col = lanes((total, total), 0), lanes((total, total), 1)
    shift, rest = split(row, n)
    step, i = split(rest, per_mate)
    pick = one_hot(col == step * per + shift + width * i)
    n_ref[:, entry:] = jnp.zeros((total, padded - entry), BF16)
    me = lax.axis_index("roll")
    sample = split(lanes((n, length_ref.shape[1]), 0), per_mate)[1]
    for copy in small:
        copy.wait()
    for s in range(width):
        length = jnp.zeros(sample.shape, jnp.int32)
        for i in range(per_mate):
            j = jnp.int32(s + width * i)
            owner = split(me + j, group)[1]
            k = prompt_at(counts_ref, owner, j)
            length = jnp.where(sample == i, len_ref[owner * prompts + k], length)
        length_ref[s * n : (s + 1) * n, :] = length
    n_ref[:, :entry] = dot(pick, f_ref[...]).astype(BF16)
    for c, copy in enumerate(copies):
        copy.wait()
        tiles = range(c * unit // 128, (c + 1) * unit // 128)
        for k in tiles:
            tall[k] = q_ref[:, k * 128 : (k + 1) * 128].astype(F32)
        for s in range(width):
            out = [
                jnp.concatenate(
                    [tall[k, pl.ds(t * per + s, per_mate, width), :] for t in range(steps)], axis=0
                )
                for k in tiles
            ]
            at = (s * heads + 2 * c) * n
            even = jnp.concatenate(out[: padded // 128], axis=1)
            odd = pltpu.roll(jnp.concatenate(out[-padded // 128 :], axis=1), entry, 1)
            o_ref[at : at + n, :] = even.astype(BF16)
            o_ref[at + n : at + 2 * n, :] = odd.astype(BF16)


def latent_kernel(geo, w_hbm, *refs):
    width, steps, per, per_mate = (geo[n] for n in ("width", "steps", "per", "per_mate"))
    halves, local, pairs, order = (geo[n] for n in ("halves", "local", "pairs", "order"))
    arrays = halves * (width + 1)
    k_hbm, refs = refs[:arrays], refs[arrays:]
    _, q_ref, n_ref, length_ref, o_hbm, keys, ctx, out, w_ref, o_ref, sems = refs
    heads, rank, dv = w_ref.shape
    half = lax.axis_index("exp")
    few = pairs * local
    sent = (len(order) - 1) * few
    piece = sent + few
    old = halves * piece
    n = per_mate * steps
    block = keys.shape[1] - old
    copies = []
    for s in range(width):
        for e in range(halves):
            first = k_hbm[e * (width + 1) + width].at[pl.ds(s * few, few)], keys.at[s, pl.ds(e * piece + sent, few)]
            rest = k_hbm[e * (width + 1) + s], keys.at[s, pl.ds(e * piece, sent)]
            for src, dst in (rest, first):
                copies.append(pltpu.make_async_copy(src, dst, sems.at[len(copies)]))
    each = len(copies) // width
    copies.append(pltpu.make_async_copy(w_hbm, w_ref, sems.at[len(copies)]))
    for copy in copies[:-1]:
        copy.start()
    _, b = split(lax.axis_index("roll"), width)
    row, col = lanes((n, old), 0), lanes((n, old), 1)
    e, rest = split(col, piece)
    rest, pos = split(rest, local)
    place, pair = split(rest, pairs)
    hop = jnp.zeros_like(place)
    for x, h in enumerate(order):
        hop = jnp.where(place == x, h, hop)
    e = e + half
    pos = jnp.where(e >= halves, e - halves, e) * local + pos
    of_carry = []
    for carry in range(2):
        other = slot_sample(geo, hop, pair, carry)
        mine = (other == split(row, per_mate)[1]) & (other < per_mate)
        of_carry.append(jnp.where(mine, pos, halves * local))
    row, col = lanes((n, block), 0), lanes((n, block), 1)
    (step, sample), (step_of, sample_of) = split(row, per_mate), split(col, per_mate)
    allowed_new = ((sample == sample_of) & (step_of <= step))[None]
    scores = []
    for s in range(width):
        query = q_ref[s * heads * n : (s + 1) * heads * n, :]
        keys[s, old : old + n, :] = n_ref[s * n : (s + 1) * n, :]
        keys[s, old + n :, :] = jnp.zeros((block - n, keys.shape[2]), BF16)
        for copy in copies[s * each : (s + 1) * each]:
            copy.wait()
        if s == 0:
            copies[-1].start()
        scores.append(dot_t(query, keys[s]).reshape(heads, n, old + block) * geo["scale"])
    weights = []
    for s in range(width):
        length = length_ref[s * n : (s + 1) * n, :]
        length = jnp.concatenate([length] * -(-old // length.shape[1]), axis=1)[:, :old]
        pos = jnp.where(b + s >= width, of_carry[1], of_carry[0])
        allowed_old = (pos < length)[None]
        part = jnp.concatenate(
            [
                jnp.where(allowed_old, scores[s][:, :, :old], NEG),
                jnp.where(allowed_new, scores[s][:, :, old:], NEG),
            ],
            axis=-1,
        )
        top = jnp.max(part, axis=-1, keepdims=True)
        raised = jnp.exp(part - top)
        part = raised / jnp.sum(raised, axis=-1, keepdims=True)
        weights.append(part.reshape(heads * n, old + block).astype(BF16))
    for s in range(width):
        context = dot(weights[s], keys[s, :, :rank]).astype(BF16)
        for h in range(heads):
            ctx[h, s * n : (s + 1) * n, :] = context[h * n : (h + 1) * n]
    copies[-1].wait()
    for h in range(heads):
        out[:, h * dv : (h + 1) * dv] = dot(ctx[h], w_ref[h]).astype(BF16)
    rows = steps * per
    shift, rest = split(lanes((rows, rows), 1), n)
    step, sample = split(rest, per_mate)
    place = step * per + shift + width * sample
    pick = one_hot(lanes((rows, rows), 0) == place)
    send = []
    for c in range(2):
        sl = pl.ds(c * (heads * dv // 2), heads * dv // 2)
        o_ref[:, sl] = dot(pick, out[:, sl]).astype(BF16)
        send.append(pltpu.make_async_copy(o_ref.at[:, sl], o_hbm.at[:, sl], sems.at[c]))
        send[c].start()
    for copy in send:
        copy.wait()


def cost(us):
    return pl.CostEstimate(
        flops=2_000_000_000 * us, bytes_accessed=3_000_000 * us, transcendentals=20_000_000 * us
    )


def call(kernel, geo, out, args, smem=0, hbm=0, after=0, scratch=(), mib=16, us=0):
    spaces = [pltpu.SMEM] * smem + [pltpu.HBM] * hbm + [pl.ANY] * after
    spaces += [pltpu.VMEM] * (len(args) - len(spaces))

    def place(x):
        if isinstance(x, jax.ShapeDtypeStruct):
            return pl.BlockSpec(memory_space=pltpu.SMEM if len(x.shape) == 1 else pltpu.VMEM)
        return pl.BlockSpec(memory_space=pltpu.HBM)

    outs = jax.tree.map(place, out)
    args = [
        pltpu.with_memory_space_constraint(x, pltpu.HBM) if s == pltpu.HBM else x
        for x, s in zip(args, spaces, strict=True)
    ]
    return pl.pallas_call(
        functools.partial(kernel, geo),
        out_shape=out,
        in_specs=[pl.BlockSpec(memory_space=s) for s in spaces],
        out_specs=outs,
        scratch_shapes=list(scratch),
        cost_estimate=cost(us),
        compiler_params=pltpu.CompilerParams(vmem_limit_bytes=mib * 1024 * 1024),
        name=kernel.__name__,
    )(*args)


def hold(x, first):
    return pl.pallas_call(
        lambda *refs: None,
        out_shape=tuple(jax.ShapeDtypeStruct(a.shape, a.dtype) for a in x),
        in_specs=[pl.BlockSpec(memory_space=pl.ANY)] * (len(x) + 1),
        out_specs=[pl.BlockSpec(memory_space=pl.ANY)] * len(x),
        input_output_aliases={n + 1: n for n in range(len(x))},
        cost_estimate=cost(20),
        name="hold",
    )(first, *x)


def pad_to(n, m):
    return -(-n // m) * m


def on_device(
    kda_prefill,
    latent_prefill,
    prompt_len,
    sample_counts,
    kda_q,
    kda_k,
    kda_v,
    kda_decay,
    kda_beta,
    mla_q,
    mla_new,
    w_uv,
):
    group = lax.axis_size("roll")
    halves = lax.axis_size("exp")
    steps, per, kda_width = kda_q.shape
    heads = kda_beta.shape[2]
    prompts, local, entry = latent_prefill.shape
    cache = local * halves
    _, rank, dv = w_uv.shape
    width = 4
    depth = group // width
    slots = -(-per // group)
    per_mate = per // width
    hops = min(depth, per_mate + 1)
    padded = pad_to(entry, 128)
    parts = max(1, min(16 // (slots * steps), heads // 2))
    geo = dict(
        group=group,
        halves=halves,
        steps=steps,
        per=per,
        width=width,
        depth=depth,
        slots=slots,
        hops=hops,
        prompts=prompts,
        cache=cache,
        entry=entry,
        per_mate=per_mate,
        local=local,
        pairs=max(-(-per_mate // depth), -(-16 // local)),
        order=[*range(1, hops), 0],
        column=[h for h in (3, 1, 2, *range(4, hops)) if h < hops],
        scale=192.0**-0.5,
        heads=heads,
        parts=parts,
    )
    shape = jax.ShapeDtypeStruct

    def mates(sign, s):
        return [(i, i // width * width + (i + sign * s) % width) for i in range(group)]

    counts = sample_counts.T
    fan = (group * parts * slots * steps, kda_width // parts)
    reads, coef, table = call(
        reads_kernel,
        geo,
        (
            shape(fan, BF16),
            shape((steps, per, kda_width), F32),
            shape((width * hops * geo["pairs"],), jnp.int32),
        ),
        (kda_q, kda_k, kda_decay, kda_v, jnp.swapaxes(kda_beta, 1, 2), counts),
        hbm=6,
        scratch=[
            pltpu.VMEM(kda_q.shape, BF16),
            pltpu.VMEM(kda_q.shape, BF16),
            pltpu.VMEM(kda_q.shape, F32),
            pltpu.VMEM(kda_q.shape, BF16),
            pltpu.VMEM((steps, heads, per), F32),
            pltpu.VMEM((steps * per * parts, kda_width // parts), BF16),
            pltpu.SMEM(counts.shape, jnp.int32),
            pltpu.SemaphoreType.DMA((3, 4)),
        ],
    )
    got = lax.all_to_all(reads, "roll", 0, 0, tiled=True)

    plane = [lax.ppermute(latent_prefill, "roll", mates(-1, s)) for s in range(1, width)]
    column = [
        lax.ppermute(latent_prefill, "roll", [(i, (i - width * h) % group) for i in range(group)])
        for h in geo["column"]
    ]
    few = geo["pairs"] * local
    sent = (hops - 1) * few
    wide = mla_q.shape[2]
    rows = steps * per
    few = geo["pairs"] * local
    sent = (hops - 1) * few
    wide = mla_q.shape[2]
    rows = steps * per
    queries, fresh, lengths = call(
        query_kernel,
        geo,
        (
            shape((heads * rows, padded), BF16),
            shape((rows, padded), BF16),
            shape((rows, 128), jnp.int32),
        ),
        (mla_q.reshape(rows, wide), mla_new.reshape(rows, entry), counts, prompt_len, reads),
        hbm=4,
        after=1,
        scratch=[
            pltpu.VMEM((rows, wide), BF16),
            pltpu.VMEM((wide // 128, rows, 128), F32),
            pltpu.VMEM((rows, entry), BF16),
            pltpu.SMEM(counts.shape, jnp.int32),
            pltpu.SMEM(prompt_len.shape, jnp.int32),
            pltpu.SemaphoreType.DMA((heads // 2 + 3,)),
        ],
    )
    chosen = call(
        select_kernel,
        geo,
        tuple(shape((sent, padded), BF16) for s in range(width)),
        (table, reads, *column),
        smem=1,
        after=1,
        us=20,
        scratch=[pltpu.VMEM(((hops - 1) * prompts, local, padded), BF16)],
    )
    products, own = call(
        state_kernel,
        geo,
        (pltpu.HBM(fan, BF16), pltpu.HBM((width * few, padded), BF16)),
        (table, kda_prefill, counts, latent_prefill, *plane, *chosen, got),
        smem=1,
        hbm=3,
        after=len(plane) + len(chosen) + 1,
        us=20,
        scratch=[
            pltpu.VMEM(fan, BF16),
            pltpu.VMEM((width * few, padded), BF16),
            pltpu.VMEM(fan, BF16),
            pltpu.VMEM(kda_prefill.shape, BF16),
            pltpu.VMEM(fan, BF16),
            pltpu.VMEM(fan, BF16),
            pltpu.VMEM((width * prompts, local, padded), BF16),
            pltpu.VMEM((width,) + latent_prefill.shape, BF16),
            pltpu.SMEM(counts.shape, jnp.int32),
            pltpu.SemaphoreType.DMA((parts + 2,)),
            pltpu.SemaphoreType.DMA((width,)),
        ],
    )
    back = lax.all_to_all(products, "roll", 0, 0, tiled=True)
    taken = [lax.ppermute(chosen[s], "roll", mates(-1, s)) for s in range(1, width)]
    taken = [*hold([chosen[0], *taken], products), own]
    caches = list(taken)
    for e in range(1, halves):
        pairs = [(i, (i - e) % halves) for i in range(halves)]
        caches += [lax.ppermute(piece, "exp", pairs) for piece in taken]
    mla_out = call(
        latent_kernel,
        geo,
        pltpu.HBM((rows, heads * dv), BF16),
        (w_uv, *caches, products, queries, fresh, lengths),
        hbm=2 + width,
        after=len(caches) - width,
        scratch=[
            pltpu.VMEM((width, hops * few * halves + pad_to(per_mate * steps, 128), padded), BF16),
            pltpu.VMEM((heads, rows, rank), BF16),
            pltpu.VMEM((rows, heads * dv), BF16),
            pltpu.VMEM(w_uv.shape, BF16),
            pltpu.VMEM((rows, heads * dv), BF16),
            pltpu.SemaphoreType.DMA((width * halves * 2 + 1,)),
        ],
    )
    kda_out = call(
        kda_out_kernel,
        geo,
        pltpu.HBM((steps, per, kda_width), BF16),
        (mla_out, pltpu.with_memory_space_constraint(back, pltpu.VMEM), coef),
        hbm=1,
        scratch=[
            pltpu.VMEM((steps, per, kda_width), BF16),
            pltpu.SemaphoreType.DMA((parts + 1,)),
        ],
    )
    return (kda_out, mla_out.reshape(steps, per, heads * dv))


def solution(mesh):
    return jax.shard_map(
        on_device,
        mesh=mesh,
        in_specs=(
            P("roll", "exp", None, None),
            P("roll", "exp", None),
            P(),
            P(),
            P(None, "roll", "exp"),
            P(None, "roll", "exp"),
            P(None, "roll", "exp"),
            P(None, "roll", "exp"),
            P(None, "roll", "exp"),
            P(None, "roll", "exp"),
            P(None, "roll", None),
            P("exp", None, None),
        ),
        out_specs=(P(None, "roll", "exp"), P(None, "roll", "exp")),
        check_vma=False,
    )
```

```python
import functools

import jax
import jax.numpy as jnp
from jax import lax
from jax.experimental import pallas as pl
from jax.experimental.pallas import tpu as pltpu
from jax.sharding import PartitionSpec as P

F32 = jnp.float32
BF16 = jnp.bfloat16
NEG = -1e30


def split(x, n):
    if n & (n - 1) == 0:
        return lax.shift_right_logical(x, jnp.full_like(x, n.bit_length() - 1)), x & (n - 1)
    return lax.div(x, jnp.full_like(x, n)), lax.rem(x, jnp.full_like(x, n))


def wrap(x, n):
    return jnp.where(x < 0, x + n, x)


def lanes(shape, dim):
    return lax.broadcasted_iota(jnp.int32, shape, dim)


def prompt_at(counts_ref, owner, j):
    bound = jnp.int32(0)
    k = jnp.zeros_like(j)
    for i in range(counts_ref.shape[0]):
        bound = bound + counts_ref[i, owner]
        k = k + (bound <= j).astype(jnp.int32)
    return k


def fan_rows(geo, shape, dim, me):
    group, slots, steps, parts, per = (geo[n] for n in ("group", "slots", "steps", "parts", "per"))
    other, rest = split(lanes(shape, dim), parts * slots * steps)
    part, rest = split(rest, slots * steps)
    slot, step = split(rest, steps)
    j = wrap(other - me, group) + group * slot
    return part, jnp.where(j < per, step * per + j, -1)


def one_hot(hit):
    return hit.astype(F32).astype(BF16)


def dot(a, b):
    return lax.dot_general(a, b, (((1,), (0,)), ((), ())), preferred_element_type=F32)


def dot_first(a, b):
    return lax.dot_general(a, b, (((0,), (0,)), ((), ())), preferred_element_type=F32)


def dot_t(a, b):
    return lax.dot_general(a, b, (((1,), (1,)), ((), ())), preferred_element_type=F32)


def row_sums(x, ones):
    return dot(x.astype(BF16), ones)


def slot_sample(geo, hop, pair, carry):
    return wrap(hop - carry, geo["depth"]) + geo["depth"] * pair


def fill_table(geo, counts_ref, table_ref):
    width, depth, prompts, pairs = (geo[n] for n in ("width", "depth", "prompts", "pairs"))
    a, b = split(lax.axis_index("roll"), width)
    at = 0
    for s in range(width):
        for hop in geo["order"]:
            if hop == 0:
                column = wrap(b + s - width, width)
                carry = (b + s >= width).astype(jnp.int32)
                owner, piece = a * width + column, s
            else:
                carry = (b < s).astype(jnp.int32)
                owner = wrap(a + hop - depth, depth) * width + b
                piece = hop - 1
            for pair in range(pairs):
                j = s + width * slot_sample(geo, hop, pair, carry)
                k = jnp.minimum(prompt_at(counts_ref, owner, j), prompts - 1)
                table_ref[at] = piece * prompts + k
                at += 1


def reads_kernel(geo, q_hbm, k_hbm, g_hbm, v_hbm, b_hbm, c_hbm, r_ref, a_ref, table_ref, *scratch):
    q_ref, k_ref, g_ref, v_ref, b_ref, raw, counts_ref, sems = scratch
    _, per, width = q_ref.shape
    heads = geo["heads"]
    dk = width // heads
    parts = geo["parts"]
    wide = width // parts
    unit = 2 * dk
    chunk = width // 2
    beta_copy = pltpu.make_async_copy(b_hbm, b_ref, sems.at[2, 0])
    beta_copy.start()
    counts_copy = pltpu.make_async_copy(c_hbm, counts_ref, sems.at[2, 1])
    counts_copy.start()
    copies = []
    for c in range(2):
        sl = pl.ds(c * chunk, chunk)
        pairs = ((q_hbm, q_ref), (k_hbm, k_ref), (g_hbm, g_ref), (v_hbm, v_ref))
        for n, (src, dst) in enumerate(pairs):
            copies.append(pltpu.make_async_copy(src.at[:, :, sl], dst.at[:, :, sl], sems.at[c, n]))
            copies[-1].start()
    me = lax.axis_index("roll")
    ones = one_hot(split(lanes((unit, unit), 0), dk)[0] == split(lanes((unit, unit), 1), dk)[0])
    rows, rows_in = r_ref.shape[0], raw.shape[0]
    part, place = fan_rows(geo, (rows, rows_in), 0, me)
    pick = one_hot((lanes((rows, rows_in), 1) == part * (2 * per) + place) & (place >= 0))
    spread = one_hot(lanes((heads, width), 0) == split(lanes((heads, width), 1), dk)[0])
    betas = []
    beta_copy.wait()
    for t in range(2):
        beta = b_ref[t]
        high = beta.astype(BF16)
        low = (beta - high.astype(F32)).astype(BF16)
        betas.append(dot_first(high, spread) + dot_first(low, spread))
    for c in range(parts):
        for at in range(c * wide, (c + 1) * wide, unit):
            if at % chunk == 0:
                for copy in copies[4 * (at // chunk) : 4 * (at // chunk) + 4]:
                    copy.wait()
            sl = slice(at, at + unit)
            q1, q2 = q_ref[0, :, sl].astype(F32), q_ref[1, :, sl].astype(F32)
            k1, k2 = k_ref[0, :, sl].astype(F32), k_ref[1, :, sl].astype(F32)
            d1, d2 = jnp.exp(-g_ref[0, :, sl]), jnp.exp(-g_ref[1, :, sl])
            dq2, dk2 = d2 * q2, d2 * k2
            terms = (q1 * q1, k1 * k1, q2 * q2, k2 * k2, k1 * q1, k2 * q2, k1 * dq2, k1 * dk2)
            sums = row_sums(jnp.concatenate(terms, axis=0), ones)
            s = [sums[n * per : (n + 1) * per] for n in range(8)]
            rq1, rk1, rq2, rk2 = (lax.rsqrt(x + 1e-06) for x in s[:4])
            b1, b2 = betas[0][:, sl], betas[1][:, sl]
            a11 = b1 * (s[4] * rk1 * rq1)
            a22 = b2 * (s[5] * rk2 * rq2)
            a22k = a22 * rk2
            a21 = b1 * (rk1 * (rq2 * s[6] - a22k * s[7]))
            r1 = d1 * (rq1 * q1 - (a11 * rk1) * k1)
            r2 = d1 * (rq2 * dq2 - a22k * dk2 - (a21 * rk1) * k1)
            to = slice(at - c * wide, at - c * wide + unit)
            raw[2 * c * per : (2 * c + 1) * per, to] = r1.astype(BF16)
            raw[(2 * c + 1) * per : (2 * c + 2) * per, to] = r2.astype(BF16)
            v1, v2 = v_ref[0, :, sl].astype(F32), v_ref[1, :, sl].astype(F32)
            a_ref[0, :, sl] = a11 * v1
            a_ref[1, :, sl] = a21 * v1 + a22 * v2
    r_ref[...] = dot(pick, raw[...]).astype(BF16)
    counts_copy.wait()
    fill_table(geo, counts_ref, table_ref)


def fill_pool(pool, pieces, prompts):
    local, entry = pieces[0].shape[1:]
    pool[:, :, entry:] = jnp.zeros(pool.shape[:2] + (pool.shape[2] - entry,), BF16)
    for n, piece in enumerate(pieces):
        pool[n * prompts : (n + 1) * prompts, :, :entry] = piece[...]


def state_kernel(geo, table_ref, s_hbm, c_hbm, own_hbm, *refs):
    pieces, refs = refs[: geo["width"] - 1], refs[-14:]
    r_hbm, y_hbm, o_hbm, y_ref, o_ref, r_ref, s_ref, r_all, y_all, pool = refs[:10]
    parts_ref, counts_ref, sems, piece_sems = refs[10:]
    pieces = [
        pltpu.make_async_copy(piece, parts_ref.at[n], piece_sems.at[n])
        for n, piece in enumerate((own_hbm, *pieces))
    ]
    rows, wide = r_ref.shape
    prompts, heads, dk, dv = s_ref.shape
    me = lax.axis_index("roll")
    group, slots, steps, parts = geo["group"], geo["slots"], geo["steps"], geo["parts"]
    first = pltpu.make_async_copy(r_hbm, r_ref, sems.at[parts + 1])
    first.start()
    copies = [pltpu.make_async_copy(c_hbm, counts_ref, sems.at[parts])]
    for c in range(parts):
        sl = pl.ds(c * (heads // parts), heads // parts)
        copies.append(pltpu.make_async_copy(s_hbm.at[:, sl], s_ref.at[:, sl], sems.at[c]))
    for copy in copies + pieces:
        copy.start()
    few, own = rows // parts, slots * steps
    part, rest = split(lanes((rows, rows), 0), few)
    other, rest = split(rest, own)
    sort = one_hot(lanes((rows, rows), 1) == (other * parts + part) * own + rest)
    part, rest = split(lanes((rows, rows), 1), few)
    other, rest = split(rest, own)
    back = one_hot(lanes((rows, rows), 0) == (other * parts + part) * own + rest)
    first.wait()
    r_all[...] = dot(sort, r_ref[...]).astype(BF16)
    copies[0].wait()
    other, rest = split(lanes((few, dk), 0), own)
    j = wrap(me - other, group) + group * split(rest, steps)[0]
    k = prompt_at(counts_ref, me, j)
    keep = [one_hot(k == p) for p in range(prompts)]
    for c in range(parts):
        copies[1 + c].wait()
        for at in range(wide // dk):
            h = c * (wide // dk) + at
            r = r_all[c * few : (c + 1) * few, at * dk : (at + 1) * dk]
            wide_r = jnp.concatenate([r * k for k in keep], axis=1)
            acc = dot(wide_r, s_ref[:, h].reshape(prompts * dk, dv))
            y_all[c * few : (c + 1) * few, at * dv : (at + 1) * dv] = acc.astype(BF16)
    y_ref[...] = dot(back, y_all[...]).astype(BF16)
    send = [pltpu.make_async_copy(y_ref, y_hbm, sems.at[0])]
    send[0].start()
    for copy in pieces:
        copy.wait()
    width, hops, pairs = geo["width"], geo["hops"], geo["pairs"]
    fill_pool(pool, [parts_ref.at[n] for n in range(width)], prompts)
    local = pool.shape[1]
    for s in range(width):
        for pair in range(pairs):
            at = (s * hops + hops - 1) * pairs + pair
            to = (s * pairs + pair) * local
            o_ref[to : to + local, :] = pool[table_ref[at]]
    send.append(pltpu.make_async_copy(o_ref, o_hbm, piece_sems.at[1]))
    send[1].start()
    for copy in send:
        copy.wait()


def kda_out_kernel(geo, _, y_ref, a_ref, o_hbm, o_ref, sems):
    per, parts = geo["per"], geo["parts"]
    rows, wide = y_ref.shape
    me = lax.axis_index("roll")
    shape = (2 * per * parts, rows)
    part, place = fan_rows(geo, shape, 1, me)
    pick = one_hot((lanes(shape, 0) == part * (2 * per) + place) & (place >= 0))
    y_all = dot(pick, y_ref[...])
    send = []
    for c in range(parts):
        sl = pl.ds(c * wide, wide)
        y = y_all[2 * c * per : 2 * (c + 1) * per]
        for t in range(2):
            o_ref[t, :, sl] = (y[t * per : (t + 1) * per] + a_ref[t, :, sl]).astype(BF16)
        if c % 2 == 1 or c == parts - 1:
            at = pl.ds(c // 2 * 2 * wide, (c % 2 + 1) * wide)
            send.append(
                pltpu.make_async_copy(o_ref.at[:, :, at], o_hbm.at[:, :, at], sems.at[1 + c])
            )
            send[-1].start()
    for copy in send:
        copy.wait()


def select_kernel(geo, table_ref, _, *refs):
    width, hops, prompts, pairs = (geo[n] for n in ("width", "hops", "prompts", "pairs"))
    pieces, o_refs, pool = refs[: hops - 1], refs[hops - 1 : -1], refs[-1]
    fill_pool(pool, [pieces[geo["column"].index(h)] for h in range(1, hops)], prompts)
    local = pool.shape[1]
    for s, o_ref in enumerate(o_refs):
        for to in range((hops - 1) * pairs):
            at = s * hops * pairs + to
            o_ref[to * local : (to + 1) * local, :] = pool[table_ref[at]]


def query_kernel(geo, q_hbm, f_hbm, c_hbm, l_hbm, _, o_ref, n_ref, length_ref, *scratch):
    q_ref, tall, f_ref, counts_ref, len_ref, sems = scratch
    total, wide = q_ref.shape
    width, per, steps, entry = geo["width"], geo["per"], geo["steps"], geo["entry"]
    group, prompts, per_mate = (geo[n] for n in ("group", "prompts", "per_mate"))
    padded = o_ref.shape[1]
    heads = wide // entry
    unit = 2 * entry
    n = total // width
    small = [
        pltpu.make_async_copy(src, dst, sems.at[heads // 2 + x])
        for x, (src, dst) in enumerate(((f_hbm, f_ref), (c_hbm, counts_ref), (l_hbm, len_ref)))
    ]
    copies = []
    for c in range(heads // 2):
        sl = pl.ds(c * unit, unit)
        copies.append(pltpu.make_async_copy(q_hbm.at[:, sl], q_ref.at[:, sl], sems.at[c]))
    for copy in small + copies:
        copy.start()
    row, col = lanes((total, total), 0), lanes((total, total), 1)
    shift, rest = split(row, n)
    step, i = split(rest, per_mate)
    pick = one_hot(col == step * per + shift + width * i)
    n_ref[:, entry:] = jnp.zeros((total, padded - entry), BF16)
    me = lax.axis_index("roll")
    sample = split(lanes((n, length_ref.shape[1]), 0), per_mate)[1]
    for copy in small:
        copy.wait()
    for s in range(width):
        length = jnp.zeros(sample.shape, jnp.int32)
        for i in range(per_mate):
            j = jnp.int32(s + width * i)
            owner = split(me + j, group)[1]
            k = prompt_at(counts_ref, owner, j)
            length = jnp.where(sample == i, len_ref[owner * prompts + k], length)
        length_ref[s * n : (s + 1) * n, :] = length
    n_ref[:, :entry] = dot(pick, f_ref[...]).astype(BF16)
    for c, copy in enumerate(copies):
        copy.wait()
        tiles = range(c * unit // 128, (c + 1) * unit // 128)
        for k in tiles:
            tall[k] = q_ref[:, k * 128 : (k + 1) * 128].astype(F32)
        for s in range(width):
            out = [
                jnp.concatenate(
                    [tall[k, pl.ds(t * per + s, per_mate, width), :] for t in range(steps)], axis=0
                )
                for k in tiles
            ]
            at = (s * heads + 2 * c) * n
            even = jnp.concatenate(out[: padded // 128], axis=1)
            odd = pltpu.roll(jnp.concatenate(out[-padded // 128 :], axis=1), entry, 1)
            o_ref[at : at + n, :] = even.astype(BF16)
            o_ref[at + n : at + 2 * n, :] = odd.astype(BF16)


def latent_kernel(geo, w_hbm, *refs):
    width, steps, per, per_mate = (geo[n] for n in ("width", "steps", "per", "per_mate"))
    halves, local, pairs, order = (geo[n] for n in ("halves", "local", "pairs", "order"))
    arrays = halves * (width + 1)
    k_hbm, refs = refs[:arrays], refs[arrays:]
    _, q_ref, n_ref, length_ref, o_hbm, keys, ctx, out, w_ref, o_ref, sems = refs
    heads, rank, dv = w_ref.shape
    half = lax.axis_index("exp")
    few = pairs * local
    sent = (len(order) - 1) * few
    piece = sent + few
    old = halves * piece
    n = per_mate * steps
    block = keys.shape[1] - old
    copies = []
    for s in range(width):
        for e in range(halves):
            first = k_hbm[e * (width + 1) + width].at[pl.ds(s * few, few)], keys.at[s, pl.ds(e * piece + sent, few)]
            rest = k_hbm[e * (width + 1) + s], keys.at[s, pl.ds(e * piece, sent)]
            for src, dst in (rest, first):
                copies.append(pltpu.make_async_copy(src, dst, sems.at[len(copies)]))
    each = len(copies) // width
    copies.append(pltpu.make_async_copy(w_hbm, w_ref, sems.at[len(copies)]))
    for copy in copies[:-1]:
        copy.start()
    _, b = split(lax.axis_index("roll"), width)
    row, col = lanes((n, old), 0), lanes((n, old), 1)
    e, rest = split(col, piece)
    rest, pos = split(rest, local)
    place, pair = split(rest, pairs)
    hop = jnp.zeros_like(place)
    for x, h in enumerate(order):
        hop = jnp.where(place == x, h, hop)
    e = e + half
    pos = jnp.where(e >= halves, e - halves, e) * local + pos
    of_carry = []
    for carry in range(2):
        other = slot_sample(geo, hop, pair, carry)
        mine = (other == split(row, per_mate)[1]) & (other < per_mate)
        of_carry.append(jnp.where(mine, pos, halves * local))
    row, col = lanes((n, block), 0), lanes((n, block), 1)
    (step, sample), (step_of, sample_of) = split(row, per_mate), split(col, per_mate)
    allowed_new = ((sample == sample_of) & (step_of <= step))[None]
    scores = []
    for s in range(width):
        query = q_ref[s * heads * n : (s + 1) * heads * n, :]
        keys[s, old : old + n, :] = n_ref[s * n : (s + 1) * n, :]
        keys[s, old + n :, :] = jnp.zeros((block - n, keys.shape[2]), BF16)
        for copy in copies[s * each : (s + 1) * each]:
            copy.wait()
        if s == 0:
            copies[-1].start()
        scores.append(dot_t(query, keys[s]).reshape(heads, n, old + block) * geo["scale"])
    weights = []
    for s in range(width):
        length = length_ref[s * n : (s + 1) * n, :]
        length = jnp.concatenate([length] * -(-old // length.shape[1]), axis=1)[:, :old]
        pos = jnp.where(b + s >= width, of_carry[1], of_carry[0])
        allowed_old = (pos < length)[None]
        part = jnp.concatenate(
            [
                jnp.where(allowed_old, scores[s][:, :, :old], NEG),
                jnp.where(allowed_new, scores[s][:, :, old:], NEG),
            ],
            axis=-1,
        )
        top = jnp.max(part, axis=-1, keepdims=True)
        raised = jnp.exp(part - top)
        part = raised / jnp.sum(raised, axis=-1, keepdims=True)
        weights.append(part.reshape(heads * n, old + block).astype(BF16))
    for s in range(width):
        context = dot(weights[s], keys[s, :, :rank]).astype(BF16)
        for h in range(heads):
            ctx[h, s * n : (s + 1) * n, :] = context[h * n : (h + 1) * n]
    copies[-1].wait()
    for h in range(heads):
        out[:, h * dv : (h + 1) * dv] = dot(ctx[h], w_ref[h]).astype(BF16)
    rows = steps * per
    shift, rest = split(lanes((rows, rows), 1), n)
    step, sample = split(rest, per_mate)
    place = step * per + shift + width * sample
    pick = one_hot(lanes((rows, rows), 0) == place)
    send = []
    for c in range(2):
        sl = pl.ds(c * (heads * dv // 2), heads * dv // 2)
        o_ref[:, sl] = dot(pick, out[:, sl]).astype(BF16)
        send.append(pltpu.make_async_copy(o_ref.at[:, sl], o_hbm.at[:, sl], sems.at[c]))
        send[c].start()
    for copy in send:
        copy.wait()


def cost(us):
    return pl.CostEstimate(
        flops=2_000_000_000 * us, bytes_accessed=3_000_000 * us, transcendentals=20_000_000 * us
    )


def call(kernel, geo, out, args, smem=0, hbm=0, after=0, scratch=(), mib=16, us=0):
    spaces = [pltpu.SMEM] * smem + [pltpu.HBM] * hbm + [pl.ANY] * after
    spaces += [pltpu.VMEM] * (len(args) - len(spaces))

    def place(x):
        if isinstance(x, jax.ShapeDtypeStruct):
            return pl.BlockSpec(memory_space=pltpu.SMEM if len(x.shape) == 1 else pltpu.VMEM)
        return pl.BlockSpec(memory_space=pltpu.HBM)

    outs = jax.tree.map(place, out)
    args = [
        pltpu.with_memory_space_constraint(x, pltpu.HBM) if s == pltpu.HBM else x
        for x, s in zip(args, spaces, strict=True)
    ]
    return pl.pallas_call(
        functools.partial(kernel, geo),
        out_shape=out,
        in_specs=[pl.BlockSpec(memory_space=s) for s in spaces],
        out_specs=outs,
        scratch_shapes=list(scratch),
        cost_estimate=cost(us),
        compiler_params=pltpu.CompilerParams(vmem_limit_bytes=mib * 1024 * 1024),
        name=kernel.__name__,
    )(*args)


def hold(x, first):
    return pl.pallas_call(
        lambda *refs: None,
        out_shape=tuple(jax.ShapeDtypeStruct(a.shape, a.dtype) for a in x),
        in_specs=[pl.BlockSpec(memory_space=pl.ANY)] * (len(x) + 1),
        out_specs=[pl.BlockSpec(memory_space=pl.ANY)] * len(x),
        input_output_aliases={n + 1: n for n in range(len(x))},
        cost_estimate=cost(20),
        name="hold",
    )(first, *x)


def pad_to(n, m):
    return -(-n // m) * m


def on_device(
    kda_prefill,
    latent_prefill,
    prompt_len,
    sample_counts,
    kda_q,
    kda_k,
    kda_v,
    kda_decay,
    kda_beta,
    mla_q,
    mla_new,
    w_uv,
):
    group = lax.axis_size("roll")
    halves = lax.axis_size("exp")
    steps, per, kda_width = kda_q.shape
    heads = kda_beta.shape[2]
    prompts, local, entry = latent_prefill.shape
    cache = local * halves
    _, rank, dv = w_uv.shape
    width = 4
    depth = group // width
    slots = -(-per // group)
    per_mate = per // width
    hops = min(depth, per_mate + 1)
    padded = pad_to(entry, 128)
    parts = max(1, min(16 // (slots * steps), heads // 2))
    geo = dict(
        group=group,
        halves=halves,
        steps=steps,
        per=per,
        width=width,
        depth=depth,
        slots=slots,
        hops=hops,
        prompts=prompts,
        cache=cache,
        entry=entry,
        per_mate=per_mate,
        local=local,
        pairs=max(-(-per_mate // depth), -(-16 // local)),
        order=[*range(1, hops), 0],
        column=[h for h in (3, 1, 2, *range(4, hops)) if h < hops],
        scale=192.0**-0.5,
        heads=heads,
        parts=parts,
    )
    shape = jax.ShapeDtypeStruct

    def mates(sign, s):
        return [(i, i // width * width + (i + sign * s) % width) for i in range(group)]

    counts = sample_counts.T
    fan = (group * parts * slots * steps, kda_width // parts)
    reads, coef, table = call(
        reads_kernel,
        geo,
        (
            shape(fan, BF16),
            shape((steps, per, kda_width), F32),
            shape((width * hops * geo["pairs"],), jnp.int32),
        ),
        (kda_q, kda_k, kda_decay, kda_v, jnp.swapaxes(kda_beta, 1, 2), counts),
        hbm=6,
        scratch=[
            pltpu.VMEM(kda_q.shape, BF16),
            pltpu.VMEM(kda_q.shape, BF16),
            pltpu.VMEM(kda_q.shape, F32),
            pltpu.VMEM(kda_q.shape, BF16),
            pltpu.VMEM((steps, heads, per), F32),
            pltpu.VMEM((steps * per * parts, kda_width // parts), BF16),
            pltpu.SMEM(counts.shape, jnp.int32),
            pltpu.SemaphoreType.DMA((3, 4)),
        ],
    )
    got = lax.all_to_all(reads, "roll", 0, 0, tiled=True)

    plane = [lax.ppermute(latent_prefill, "roll", mates(-1, s)) for s in range(1, width)]
    column = [
        lax.ppermute(latent_prefill, "roll", [(i, (i - width * h) % group) for i in range(group)])
        for h in geo["column"]
    ]
    few = geo["pairs"] * local
    sent = (hops - 1) * few
    wide = mla_q.shape[2]
    rows = steps * per
    few = geo["pairs"] * local
    sent = (hops - 1) * few
    wide = mla_q.shape[2]
    rows = steps * per
    queries, fresh, lengths = call(
        query_kernel,
        geo,
        (
            shape((heads * rows, padded), BF16),
            shape((rows, padded), BF16),
            shape((rows, 128), jnp.int32),
        ),
        (mla_q.reshape(rows, wide), mla_new.reshape(rows, entry), counts, prompt_len, reads),
        hbm=4,
        after=1,
        scratch=[
            pltpu.VMEM((rows, wide), BF16),
            pltpu.VMEM((wide // 128, rows, 128), F32),
            pltpu.VMEM((rows, entry), BF16),
            pltpu.SMEM(counts.shape, jnp.int32),
            pltpu.SMEM(prompt_len.shape, jnp.int32),
            pltpu.SemaphoreType.DMA((heads // 2 + 3,)),
        ],
    )
    chosen = call(
        select_kernel,
        geo,
        tuple(shape((sent, padded), BF16) for s in range(width)),
        (table, reads, *column),
        smem=1,
        after=1,
        us=20,
        scratch=[pltpu.VMEM(((hops - 1) * prompts, local, padded), BF16)],
    )
    products, own = call(
        state_kernel,
        geo,
        (pltpu.HBM(fan, BF16), pltpu.HBM((width * few, padded), BF16)),
        (table, kda_prefill, counts, latent_prefill, *plane, *chosen, got),
        smem=1,
        hbm=3,
        after=len(plane) + len(chosen) + 1,
        us=20,
        scratch=[
            pltpu.VMEM(fan, BF16),
            pltpu.VMEM((width * few, padded), BF16),
            pltpu.VMEM(fan, BF16),
            pltpu.VMEM(kda_prefill.shape, BF16),
            pltpu.VMEM(fan, BF16),
            pltpu.VMEM(fan, BF16),
            pltpu.VMEM((width * prompts, local, padded), BF16),
            pltpu.VMEM((width,) + latent_prefill.shape, BF16),
            pltpu.SMEM(counts.shape, jnp.int32),
            pltpu.SemaphoreType.DMA((parts + 2,)),
            pltpu.SemaphoreType.DMA((width,)),
        ],
    )
    back = lax.all_to_all(products, "roll", 0, 0, tiled=True)
    taken = [lax.ppermute(chosen[s], "roll", mates(-1, s)) for s in range(1, width)]
    taken = [*hold([chosen[0], *taken], products), own]
    caches = list(taken)
    for e in range(1, halves):
        pairs = [(i, (i - e) % halves) for i in range(halves)]
        caches += [lax.ppermute(piece, "exp", pairs) for piece in taken]
    mla_out = call(
        latent_kernel,
        geo,
        pltpu.HBM((rows, heads * dv), BF16),
        (w_uv, *caches, products, queries, fresh, lengths),
        hbm=2 + width,
        after=len(caches) - width,
        scratch=[
            pltpu.VMEM((width, hops * few * halves + pad_to(per_mate * steps, 128), padded), BF16),
            pltpu.VMEM((heads, rows, rank), BF16),
            pltpu.VMEM((rows, heads * dv), BF16),
            pltpu.VMEM(w_uv.shape, BF16),
            pltpu.VMEM((rows, heads * dv), BF16),
            pltpu.SemaphoreType.DMA((width * halves * 2 + 1,)),
        ],
    )
    kda_out = call(
        kda_out_kernel,
        geo,
        pltpu.HBM((steps, per, kda_width), BF16),
        (mla_out, pltpu.with_memory_space_constraint(back, pltpu.VMEM), coef),
        hbm=1,
        scratch=[
            pltpu.VMEM((steps, per, kda_width), BF16),
            pltpu.SemaphoreType.DMA((parts + 1,)),
        ],
    )
    return (kda_out, mla_out.reshape(steps, per, heads * dv))


def solution(mesh):
    return jax.shard_map(
        on_device,
        mesh=mesh,
        in_specs=(
            P("roll", "exp", None, None),
            P("roll", "exp", None),
            P(),
            P(),
            P(None, "roll", "exp"),
            P(None, "roll", "exp"),
            P(None, "roll", "exp"),
            P(None, "roll", "exp"),
            P(None, "roll", "exp"),
            P(None, "roll", "exp"),
            P(None, "roll", None),
            P("exp", None, None),
        ),
        out_specs=(P(None, "roll", "exp"), P(None, "roll", "exp")),
        check_vma=False,
    )
```

```python
import functools

import jax
import jax.numpy as jnp
from jax import lax
from jax.experimental import pallas as pl
from jax.experimental.pallas import tpu as pltpu
from jax.sharding import PartitionSpec as P

F32 = jnp.float32
BF16 = jnp.bfloat16
NEG = -1e30


def split(x, n):
    if n & (n - 1) == 0:
        return lax.shift_right_logical(x, jnp.full_like(x, n.bit_length() - 1)), x & (n - 1)
    return lax.div(x, jnp.full_like(x, n)), lax.rem(x, jnp.full_like(x, n))


def wrap(x, n):
    return jnp.where(x < 0, x + n, x)


def lanes(shape, dim):
    return lax.broadcasted_iota(jnp.int32, shape, dim)


def prompt_at(counts_ref, owner, j):
    bound = jnp.int32(0)
    k = jnp.zeros_like(j)
    for i in range(counts_ref.shape[0]):
        bound = bound + counts_ref[i, owner]
        k = k + (bound <= j).astype(jnp.int32)
    return k


def fan_rows(geo, shape, dim, me):
    group, slots, steps, parts, per = (geo[n] for n in ("group", "slots", "steps", "parts", "per"))
    other, rest = split(lanes(shape, dim), parts * slots * steps)
    part, rest = split(rest, slots * steps)
    slot, step = split(rest, steps)
    j = wrap(other - me, group) + group * slot
    return part, jnp.where(j < per, step * per + j, -1)


def one_hot(hit):
    return hit.astype(F32).astype(BF16)


def dot(a, b):
    return lax.dot_general(a, b, (((1,), (0,)), ((), ())), preferred_element_type=F32)


def dot_first(a, b):
    return lax.dot_general(a, b, (((0,), (0,)), ((), ())), preferred_element_type=F32)


def dot_t(a, b):
    return lax.dot_general(a, b, (((1,), (1,)), ((), ())), preferred_element_type=F32)


def row_sums(x, ones):
    return dot(x.astype(BF16), ones)


def slot_sample(geo, hop, pair, carry):
    return wrap(hop - carry, geo["depth"]) + geo["depth"] * pair


def fill_table(geo, counts_ref, table_ref):
    width, depth, prompts, pairs = (geo[n] for n in ("width", "depth", "prompts", "pairs"))
    a, b = split(lax.axis_index("roll"), width)
    at = 0
    for s in range(width):
        for hop in geo["order"]:
            if hop == 0:
                column = wrap(b + s - width, width)
                carry = (b + s >= width).astype(jnp.int32)
                owner, piece = a * width + column, s
            else:
                carry = (b < s).astype(jnp.int32)
                owner = wrap(a + hop - depth, depth) * width + b
                piece = hop - 1
            for pair in range(pairs):
                j = s + width * slot_sample(geo, hop, pair, carry)
                k = jnp.minimum(prompt_at(counts_ref, owner, j), prompts - 1)
                table_ref[at] = piece * prompts + k
                at += 1


def reads_kernel(geo, q_hbm, k_hbm, g_hbm, v_hbm, b_hbm, c_hbm, r_ref, a_ref, table_ref, *scratch):
    q_ref, k_ref, g_ref, v_ref, b_ref, raw, counts_ref, sems = scratch
    _, per, width = q_ref.shape
    heads = geo["heads"]
    dk = width // heads
    parts = geo["parts"]
    wide = width // parts
    unit = 2 * dk
    chunk = width // 2
    beta_copy = pltpu.make_async_copy(b_hbm, b_ref, sems.at[2, 0])
    beta_copy.start()
    counts_copy = pltpu.make_async_copy(c_hbm, counts_ref, sems.at[2, 1])
    counts_copy.start()
    copies = []
    for c in range(2):
        sl = pl.ds(c * chunk, chunk)
        pairs = ((q_hbm, q_ref), (k_hbm, k_ref), (g_hbm, g_ref), (v_hbm, v_ref))
        for n, (src, dst) in enumerate(pairs):
            copies.append(pltpu.make_async_copy(src.at[:, :, sl], dst.at[:, :, sl], sems.at[c, n]))
            copies[-1].start()
    me = lax.axis_index("roll")
    ones = one_hot(split(lanes((unit, unit), 0), dk)[0] == split(lanes((unit, unit), 1), dk)[0])
    rows, rows_in = r_ref.shape[0], raw.shape[0]
    part, place = fan_rows(geo, (rows, rows_in), 0, me)
    pick = one_hot((lanes((rows, rows_in), 1) == part * (2 * per) + place) & (place >= 0))
    spread = one_hot(lanes((heads, width), 0) == split(lanes((heads, width), 1), dk)[0])
    betas = []
    beta_copy.wait()
    for t in range(2):
        beta = b_ref[t]
        high = beta.astype(BF16)
        low = (beta - high.astype(F32)).astype(BF16)
        betas.append(dot_first(high, spread) + dot_first(low, spread))
    for c in range(parts):
        for at in range(c * wide, (c + 1) * wide, unit):
            if at % chunk == 0:
                for copy in copies[4 * (at // chunk) : 4 * (at // chunk) + 4]:
                    copy.wait()
            sl = slice(at, at + unit)
            q1, q2 = q_ref[0, :, sl].astype(F32), q_ref[1, :, sl].astype(F32)
            k1, k2 = k_ref[0, :, sl].astype(F32), k_ref[1, :, sl].astype(F32)
            d1, d2 = jnp.exp(-g_ref[0, :, sl]), jnp.exp(-g_ref[1, :, sl])
            dq2, dk2 = d2 * q2, d2 * k2
            terms = (q1 * q1, k1 * k1, q2 * q2, k2 * k2, k1 * q1, k2 * q2, k1 * dq2, k1 * dk2)
            sums = row_sums(jnp.concatenate(terms, axis=0), ones)
            s = [sums[n * per : (n + 1) * per] for n in range(8)]
            rq1, rk1, rq2, rk2 = (lax.rsqrt(x + 1e-06) for x in s[:4])
            b1, b2 = betas[0][:, sl], betas[1][:, sl]
            a11 = b1 * (s[4] * rk1 * rq1)
            a22 = b2 * (s[5] * rk2 * rq2)
            a22k = a22 * rk2
            a21 = b1 * (rk1 * (rq2 * s[6] - a22k * s[7]))
            r1 = d1 * (rq1 * q1 - (a11 * rk1) * k1)
            r2 = d1 * (rq2 * dq2 - a22k * dk2 - (a21 * rk1) * k1)
            to = slice(at - c * wide, at - c * wide + unit)
            raw[2 * c * per : (2 * c + 1) * per, to] = r1.astype(BF16)
            raw[(2 * c + 1) * per : (2 * c + 2) * per, to] = r2.astype(BF16)
            v1, v2 = v_ref[0, :, sl].astype(F32), v_ref[1, :, sl].astype(F32)
            a_ref[0, :, sl] = a11 * v1
            a_ref[1, :, sl] = a21 * v1 + a22 * v2
    r_ref[...] = dot(pick, raw[...]).astype(BF16)
    counts_copy.wait()
    fill_table(geo, counts_ref, table_ref)


def fill_pool(pool, pieces, prompts):
    local, entry = pieces[0].shape[1:]
    pool[:, :, entry:] = jnp.zeros(pool.shape[:2] + (pool.shape[2] - entry,), BF16)
    for n, piece in enumerate(pieces):
        pool[n * prompts : (n + 1) * prompts, :, :entry] = piece[...]


def state_kernel(geo, table_ref, s_hbm, c_hbm, own_hbm, *refs):
    pieces, refs = refs[: geo["width"] - 1], refs[-14:]
    r_hbm, y_hbm, o_hbm, y_ref, o_ref, r_ref, s_ref, r_all, y_all, pool = refs[:10]
    parts_ref, counts_ref, sems, piece_sems = refs[10:]
    pieces = [
        pltpu.make_async_copy(piece, parts_ref.at[n], piece_sems.at[n])
        for n, piece in enumerate((own_hbm, *pieces))
    ]
    rows, wide = r_ref.shape
    prompts, heads, dk, dv = s_ref.shape
    me = lax.axis_index("roll")
    group, slots, steps, parts = geo["group"], geo["slots"], geo["steps"], geo["parts"]
    first = pltpu.make_async_copy(r_hbm, r_ref, sems.at[parts + 1])
    first.start()
    copies = [pltpu.make_async_copy(c_hbm, counts_ref, sems.at[parts])]
    for c in range(parts):
        sl = pl.ds(c * (heads // parts), heads // parts)
        copies.append(pltpu.make_async_copy(s_hbm.at[:, sl], s_ref.at[:, sl], sems.at[c]))
    for copy in copies + pieces:
        copy.start()
    few, own = rows // parts, slots * steps
    part, rest = split(lanes((rows, rows), 0), few)
    other, rest = split(rest, own)
    sort = one_hot(lanes((rows, rows), 1) == (other * parts + part) * own + rest)
    part, rest = split(lanes((rows, rows), 1), few)
    other, rest = split(rest, own)
    back = one_hot(lanes((rows, rows), 0) == (other * parts + part) * own + rest)
    first.wait()
    r_all[...] = dot(sort, r_ref[...]).astype(BF16)
    copies[0].wait()
    other, rest = split(lanes((few, dk), 0), own)
    j = wrap(me - other, group) + group * split(rest, steps)[0]
    k = prompt_at(counts_ref, me, j)
    keep = [one_hot(k == p) for p in range(prompts)]
    for c in range(parts):
        copies[1 + c].wait()
        for at in range(wide // dk):
            h = c * (wide // dk) + at
            r = r_all[c * few : (c + 1) * few, at * dk : (at + 1) * dk]
            wide_r = jnp.concatenate([r * k for k in keep], axis=1)
            acc = dot(wide_r, s_ref[:, h].reshape(prompts * dk, dv))
            y_all[c * few : (c + 1) * few, at * dv : (at + 1) * dv] = acc.astype(BF16)
    y_ref[...] = dot(back, y_all[...]).astype(BF16)
    send = [pltpu.make_async_copy(y_ref, y_hbm, sems.at[0])]
    send[0].start()
    for copy in pieces:
        copy.wait()
    width, hops, pairs = geo["width"], geo["hops"], geo["pairs"]
    fill_pool(pool, [parts_ref.at[n] for n in range(width)], prompts)
    local = pool.shape[1]
    for s in range(width):
        for pair in range(pairs):
            at = (s * hops + hops - 1) * pairs + pair
            to = (s * pairs + pair) * local
            o_ref[to : to + local, :] = pool[table_ref[at]]
    send.append(pltpu.make_async_copy(o_ref, o_hbm, piece_sems.at[1]))
    send[1].start()
    for copy in send:
        copy.wait()


def kda_out_kernel(geo, _, y_ref, a_ref, o_hbm, o_ref, sems):
    per, parts = geo["per"], geo["parts"]
    rows, wide = y_ref.shape
    me = lax.axis_index("roll")
    shape = (2 * per * parts, rows)
    part, place = fan_rows(geo, shape, 1, me)
    pick = one_hot((lanes(shape, 0) == part * (2 * per) + place) & (place >= 0))
    y_all = dot(pick, y_ref[...])
    send = []
    for c in range(parts):
        sl = pl.ds(c * wide, wide)
        y = y_all[2 * c * per : 2 * (c + 1) * per]
        for t in range(2):
            o_ref[t, :, sl] = (y[t * per : (t + 1) * per] + a_ref[t, :, sl]).astype(BF16)
        if c % 2 == 1 or c == parts - 1:
            at = pl.ds(c // 2 * 2 * wide, (c % 2 + 1) * wide)
            send.append(
                pltpu.make_async_copy(o_ref.at[:, :, at], o_hbm.at[:, :, at], sems.at[1 + c])
            )
            send[-1].start()
    for copy in send:
        copy.wait()


def select_kernel(geo, table_ref, _, *refs):
    width, hops, prompts, pairs = (geo[n] for n in ("width", "hops", "prompts", "pairs"))
    pieces, o_refs, pool = refs[: hops - 1], refs[hops - 1 : -1], refs[-1]
    fill_pool(pool, [pieces[geo["column"].index(h)] for h in range(1, hops)], prompts)
    local = pool.shape[1]
    for s, o_ref in enumerate(o_refs):
        for to in range((hops - 1) * pairs):
            at = s * hops * pairs + to
            o_ref[to * local : (to + 1) * local, :] = pool[table_ref[at]]


def query_kernel(geo, q_hbm, f_hbm, c_hbm, l_hbm, _, o_ref, n_ref, length_ref, *scratch):
    q_ref, tall, f_ref, counts_ref, len_ref, sems = scratch
    total, wide = q_ref.shape
    width, per, steps, entry = geo["width"], geo["per"], geo["steps"], geo["entry"]
    group, prompts, per_mate = (geo[n] for n in ("group", "prompts", "per_mate"))
    padded = o_ref.shape[1]
    heads = wide // entry
    unit = 2 * entry
    n = total // width
    small = [
        pltpu.make_async_copy(src, dst, sems.at[heads // 2 + x])
        for x, (src, dst) in enumerate(((f_hbm, f_ref), (c_hbm, counts_ref), (l_hbm, len_ref)))
    ]
    copies = []
    for c in range(heads // 2):
        sl = pl.ds(c * unit, unit)
        copies.append(pltpu.make_async_copy(q_hbm.at[:, sl], q_ref.at[:, sl], sems.at[c]))
    for copy in small + copies:
        copy.start()
    row, col = lanes((total, total), 0), lanes((total, total), 1)
    shift, rest = split(row, n)
    step, i = split(rest, per_mate)
    pick = one_hot(col == step * per + shift + width * i)
    n_ref[:, entry:] = jnp.zeros((total, padded - entry), BF16)
    me = lax.axis_index("roll")
    sample = split(lanes((n, length_ref.shape[1]), 0), per_mate)[1]
    for copy in small:
        copy.wait()
    for s in range(width):
        length = jnp.zeros(sample.shape, jnp.int32)
        for i in range(per_mate):
            j = jnp.int32(s + width * i)
            owner = split(me + j, group)[1]
            k = prompt_at(counts_ref, owner, j)
            length = jnp.where(sample == i, len_ref[owner * prompts + k], length)
        length_ref[s * n : (s + 1) * n, :] = length
    n_ref[:, :entry] = dot(pick, f_ref[...]).astype(BF16)
    for c, copy in enumerate(copies):
        copy.wait()
        tiles = range(c * unit // 128, (c + 1) * unit // 128)
        for k in tiles:
            tall[k] = q_ref[:, k * 128 : (k + 1) * 128].astype(F32)
        for s in range(width):
            out = [
                jnp.concatenate(
                    [tall[k, pl.ds(t * per + s, per_mate, width), :] for t in range(steps)], axis=0
                )
                for k in tiles
            ]
            at = (s * heads + 2 * c) * n
            even = jnp.concatenate(out[: padded // 128], axis=1)
            odd = pltpu.roll(jnp.concatenate(out[-padded // 128 :], axis=1), entry, 1)
            o_ref[at : at + n, :] = even.astype(BF16)
            o_ref[at + n : at + 2 * n, :] = odd.astype(BF16)


def latent_kernel(geo, w_hbm, *refs):
    width, steps, per, per_mate = (geo[n] for n in ("width", "steps", "per", "per_mate"))
    halves, local, pairs, order = (geo[n] for n in ("halves", "local", "pairs", "order"))
    arrays = halves * (width + 1)
    k_hbm, refs = refs[:arrays], refs[arrays:]
    _, q_ref, n_ref, length_ref, o_hbm, keys, ctx, out, w_ref, o_ref, sems = refs
    heads, rank, dv = w_ref.shape
    half = lax.axis_index("exp")
    few = pairs * local
    sent = (len(order) - 1) * few
    piece = sent + few
    old = halves * piece
    n = per_mate * steps
    block = keys.shape[1] - old
    copies = []
    for s in range(width):
        for e in range(halves):
            first = k_hbm[e * (width + 1) + width].at[pl.ds(s * few, few)], keys.at[s, pl.ds(e * piece + sent, few)]
            rest = k_hbm[e * (width + 1) + s], keys.at[s, pl.ds(e * piece, sent)]
            for src, dst in (rest, first):
                copies.append(pltpu.make_async_copy(src, dst, sems.at[len(copies)]))
    each = len(copies) // width
    copies.append(pltpu.make_async_copy(w_hbm, w_ref, sems.at[len(copies)]))
    for copy in copies[:-1]:
        copy.start()
    _, b = split(lax.axis_index("roll"), width)
    row, col = lanes((n, old), 0), lanes((n, old), 1)
    e, rest = split(col, piece)
    rest, pos = split(rest, local)
    place, pair = split(rest, pairs)
    hop = jnp.zeros_like(place)
    for x, h in enumerate(order):
        hop = jnp.where(place == x, h, hop)
    e = e + half
    pos = jnp.where(e >= halves, e - halves, e) * local + pos
    of_carry = []
    for carry in range(2):
        other = slot_sample(geo, hop, pair, carry)
        mine = (other == split(row, per_mate)[1]) & (other < per_mate)
        of_carry.append(jnp.where(mine, pos, halves * local))
    row, col = lanes((n, block), 0), lanes((n, block), 1)
    (step, sample), (step_of, sample_of) = split(row, per_mate), split(col, per_mate)
    allowed_new = ((sample == sample_of) & (step_of <= step))[None]
    scores = []
    for s in range(width):
        query = q_ref[s * heads * n : (s + 1) * heads * n, :]
        keys[s, old : old + n, :] = n_ref[s * n : (s + 1) * n, :]
        keys[s, old + n :, :] = jnp.zeros((block - n, keys.shape[2]), BF16)
        for copy in copies[s * each : (s + 1) * each]:
            copy.wait()
        if s == 0:
            copies[-1].start()
        scores.append(dot_t(query, keys[s]).reshape(heads, n, old + block) * geo["scale"])
    weights = []
    for s in range(width):
        length = length_ref[s * n : (s + 1) * n, :]
        length = jnp.concatenate([length] * -(-old // length.shape[1]), axis=1)[:, :old]
        pos = jnp.where(b + s >= width, of_carry[1], of_carry[0])
        allowed_old = (pos < length)[None]
        part = jnp.concatenate(
            [
                jnp.where(allowed_old, scores[s][:, :, :old], NEG),
                jnp.where(allowed_new, scores[s][:, :, old:], NEG),
            ],
            axis=-1,
        )
        top = jnp.max(part, axis=-1, keepdims=True)
        raised = jnp.exp(part - top)
        part = raised / jnp.sum(raised, axis=-1, keepdims=True)
        weights.append(part.reshape(heads * n, old + block).astype(BF16))
    for s in range(width):
        context = dot(weights[s], keys[s, :, :rank]).astype(BF16)
        for h in range(heads):
            ctx[h, s * n : (s + 1) * n, :] = context[h * n : (h + 1) * n]
    copies[-1].wait()
    for h in range(heads):
        out[:, h * dv : (h + 1) * dv] = dot(ctx[h], w_ref[h]).astype(BF16)
    rows = steps * per
    shift, rest = split(lanes((rows, rows), 1), n)
    step, sample = split(rest, per_mate)
    place = step * per + shift + width * sample
    pick = one_hot(lanes((rows, rows), 0) == place)
    send = []
    for c in range(2):
        sl = pl.ds(c * (heads * dv // 2), heads * dv // 2)
        o_ref[:, sl] = dot(pick, out[:, sl]).astype(BF16)
        send.append(pltpu.make_async_copy(o_ref.at[:, sl], o_hbm.at[:, sl], sems.at[c]))
        send[c].start()
    for copy in send:
        copy.wait()


def cost(us):
    return pl.CostEstimate(
        flops=2_000_000_000 * us, bytes_accessed=3_000_000 * us, transcendentals=20_000_000 * us
    )


def call(kernel, geo, out, args, smem=0, hbm=0, after=0, scratch=(), mib=16, us=0):
    spaces = [pltpu.SMEM] * smem + [pltpu.HBM] * hbm + [pl.ANY] * after
    spaces += [pltpu.VMEM] * (len(args) - len(spaces))

    def place(x):
        if isinstance(x, jax.ShapeDtypeStruct):
            return pl.BlockSpec(memory_space=pltpu.SMEM if len(x.shape) == 1 else pltpu.VMEM)
        return pl.BlockSpec(memory_space=pltpu.HBM)

    outs = jax.tree.map(place, out)
    args = [
        pltpu.with_memory_space_constraint(x, pltpu.HBM) if s == pltpu.HBM else x
        for x, s in zip(args, spaces, strict=True)
    ]
    return pl.pallas_call(
        functools.partial(kernel, geo),
        out_shape=out,
        in_specs=[pl.BlockSpec(memory_space=s) for s in spaces],
        out_specs=outs,
        scratch_shapes=list(scratch),
        cost_estimate=cost(us),
        compiler_params=pltpu.CompilerParams(vmem_limit_bytes=mib * 1024 * 1024),
        name=kernel.__name__,
    )(*args)


def hold(x, first):
    return pl.pallas_call(
        lambda *refs: None,
        out_shape=tuple(jax.ShapeDtypeStruct(a.shape, a.dtype) for a in x),
        in_specs=[pl.BlockSpec(memory_space=pl.ANY)] * (len(x) + 1),
        out_specs=[pl.BlockSpec(memory_space=pl.ANY)] * len(x),
        input_output_aliases={n + 1: n for n in range(len(x))},
        cost_estimate=cost(20),
        name="hold",
    )(first, *x)


def pad_to(n, m):
    return -(-n // m) * m


def on_device(
    kda_prefill,
    latent_prefill,
    prompt_len,
    sample_counts,
    kda_q,
    kda_k,
    kda_v,
    kda_decay,
    kda_beta,
    mla_q,
    mla_new,
    w_uv,
):
    group = lax.axis_size("roll")
    halves = lax.axis_size("exp")
    steps, per, kda_width = kda_q.shape
    heads = kda_beta.shape[2]
    prompts, local, entry = latent_prefill.shape
    cache = local * halves
    _, rank, dv = w_uv.shape
    width = 4
    depth = group // width
    slots = -(-per // group)
    per_mate = per // width
    hops = min(depth, per_mate + 1)
    padded = pad_to(entry, 128)
    parts = max(1, min(16 // (slots * steps), heads // 2))
    geo = dict(
        group=group,
        halves=halves,
        steps=steps,
        per=per,
        width=width,
        depth=depth,
        slots=slots,
        hops=hops,
        prompts=prompts,
        cache=cache,
        entry=entry,
        per_mate=per_mate,
        local=local,
        pairs=max(-(-per_mate // depth), -(-16 // local)),
        order=[*range(1, hops), 0],
        column=[h for h in (3, 1, 2, *range(4, hops)) if h < hops],
        scale=192.0**-0.5,
        heads=heads,
        parts=parts,
    )
    shape = jax.ShapeDtypeStruct

    def mates(sign, s):
        return [(i, i // width * width + (i + sign * s) % width) for i in range(group)]

    counts = sample_counts.T
    fan = (group * parts * slots * steps, kda_width // parts)
    reads, coef, table = call(
        reads_kernel,
        geo,
        (
            shape(fan, BF16),
            shape((steps, per, kda_width), F32),
            shape((width * hops * geo["pairs"],), jnp.int32),
        ),
        (kda_q, kda_k, kda_decay, kda_v, jnp.swapaxes(kda_beta, 1, 2), counts),
        hbm=6,
        scratch=[
            pltpu.VMEM(kda_q.shape, BF16),
            pltpu.VMEM(kda_q.shape, BF16),
            pltpu.VMEM(kda_q.shape, F32),
            pltpu.VMEM(kda_q.shape, BF16),
            pltpu.VMEM((steps, heads, per), F32),
            pltpu.VMEM((steps * per * parts, kda_width // parts), BF16),
            pltpu.SMEM(counts.shape, jnp.int32),
            pltpu.SemaphoreType.DMA((3, 4)),
        ],
    )
    got = lax.all_to_all(reads, "roll", 0, 0, tiled=True)

    plane = [lax.ppermute(latent_prefill, "roll", mates(-1, s)) for s in range(1, width)]
    column = [
        lax.ppermute(latent_prefill, "roll", [(i, (i - width * h) % group) for i in range(group)])
        for h in geo["column"]
    ]
    few = geo["pairs"] * local
    sent = (hops - 1) * few
    wide = mla_q.shape[2]
    rows = steps * per
    few = geo["pairs"] * local
    sent = (hops - 1) * few
    wide = mla_q.shape[2]
    rows = steps * per
    queries, fresh, lengths = call(
        query_kernel,
        geo,
        (
            shape((heads * rows, padded), BF16),
            shape((rows, padded), BF16),
            shape((rows, 128), jnp.int32),
        ),
        (mla_q.reshape(rows, wide), mla_new.reshape(rows, entry), counts, prompt_len, reads),
        hbm=4,
        after=1,
        scratch=[
            pltpu.VMEM((rows, wide), BF16),
            pltpu.VMEM((wide // 128, rows, 128), F32),
            pltpu.VMEM((rows, entry), BF16),
            pltpu.SMEM(counts.shape, jnp.int32),
            pltpu.SMEM(prompt_len.shape, jnp.int32),
            pltpu.SemaphoreType.DMA((heads // 2 + 3,)),
        ],
    )
    chosen = call(
        select_kernel,
        geo,
        tuple(shape((sent, padded), BF16) for s in range(width)),
        (table, reads, *column),
        smem=1,
        after=1,
        us=20,
        scratch=[pltpu.VMEM(((hops - 1) * prompts, local, padded), BF16)],
    )
    products, own = call(
        state_kernel,
        geo,
        (pltpu.HBM(fan, BF16), pltpu.HBM((width * few, padded), BF16)),
        (table, kda_prefill, counts, latent_prefill, *plane, *chosen, got),
        smem=1,
        hbm=3,
        after=len(plane) + len(chosen) + 1,
        us=20,
        scratch=[
            pltpu.VMEM(fan, BF16),
            pltpu.VMEM((width * few, padded), BF16),
            pltpu.VMEM(fan, BF16),
            pltpu.VMEM(kda_prefill.shape, BF16),
            pltpu.VMEM(fan, BF16),
            pltpu.VMEM(fan, BF16),
            pltpu.VMEM((width * prompts, local, padded), BF16),
            pltpu.VMEM((width,) + latent_prefill.shape, BF16),
            pltpu.SMEM(counts.shape, jnp.int32),
            pltpu.SemaphoreType.DMA((parts + 2,)),
            pltpu.SemaphoreType.DMA((width,)),
        ],
    )
    back = lax.all_to_all(products, "roll", 0, 0, tiled=True)
    taken = [lax.ppermute(chosen[s], "roll", mates(-1, s)) for s in range(1, width)]
    taken = [chosen[0], *hold(taken, products), own]
    caches = list(taken)
    for e in range(1, halves):
        pairs = [(i, (i - e) % halves) for i in range(halves)]
        caches += [lax.ppermute(piece, "exp", pairs) for piece in taken]
    mla_out = call(
        latent_kernel,
        geo,
        pltpu.HBM((rows, heads * dv), BF16),
        (w_uv, *caches, products, queries, fresh, lengths),
        hbm=2 + width,
        after=len(caches) - width,
        scratch=[
            pltpu.VMEM((width, hops * few * halves + pad_to(per_mate * steps, 128), padded), BF16),
            pltpu.VMEM((heads, rows, rank), BF16),
            pltpu.VMEM((rows, heads * dv), BF16),
            pltpu.VMEM(w_uv.shape, BF16),
            pltpu.VMEM((rows, heads * dv), BF16),
            pltpu.SemaphoreType.DMA((width * halves * 2 + 1,)),
        ],
    )
    kda_out = call(
        kda_out_kernel,
        geo,
        pltpu.HBM((steps, per, kda_width), BF16),
        (mla_out, pltpu.with_memory_space_constraint(back, pltpu.VMEM), coef),
        hbm=1,
        scratch=[
            pltpu.VMEM((steps, per, kda_width), BF16),
            pltpu.SemaphoreType.DMA((parts + 1,)),
        ],
    )
    return (kda_out, mla_out.reshape(steps, per, heads * dv))


def solution(mesh):
    return jax.shard_map(
        on_device,
        mesh=mesh,
        in_specs=(
            P("roll", "exp", None, None),
            P("roll", "exp", None),
            P(),
            P(),
            P(None, "roll", "exp"),
            P(None, "roll", "exp"),
            P(None, "roll", "exp"),
            P(None, "roll", "exp"),
            P(None, "roll", "exp"),
            P(None, "roll", "exp"),
            P(None, "roll", None),
            P("exp", None, None),
        ),
        out_specs=(P(None, "roll", "exp"), P(None, "roll", "exp")),
        check_vma=False,
    )
```
